128 devices in a mesh: layer: 8 (over z_lo, y), latent: 16 (over x, z_hi, core).
Axes of the slice: x: 4, y: 4, z: 4 (z_hi: 2, z_lo: 2; z = z_hi * 2 + z_lo), core: 2. Of those that a mesh axis runs over, the one named last changes fastest.
Arguments:
- acts: bfloat16 [1024, 8, 2048], P('latent', 'layer'), may hold values from -6 to 6
- enc_weight: bfloat16 [8, 2048, 16384], P('layer', None, 'latent'), may hold values from -0.046875 to 0.046875
- enc_bias: float32 [16384], P('latent'), may hold values from -1 to 0.5
- dec_weight: bfloat16 [16384, 8, 2048], P('latent', 'layer'), may hold values from -2 to 2
- dec_bias: float32 [8, 2048], P('layer'), may hold values from -3 to 3
Outputs:
- enc_grad: float32 [8, 2048, 16384], P('layer', None, 'latent')
- enc_bias_grad: float32 [16384], P('latent')
- dec_grad: float32 [16384, 8, 2048], P('latent', 'layer')
- dec_bias_grad: float32 [8, 2048], P('layer')
The draws below stay inside these ranges and needn't reach their ends.
All inputs are finite; a program needn't handle non-finite values.
Results may differ from the reference program's by a relative error of at most 0.0041.
Values may be sent and summed in bfloat16 or wider, within the bound.
A program may use at most 128 MiB of HBM per device.

```python
import math
import jax
import jax.numpy as jnp
from jax import lax

D = 2048
L = 8
F = 16384
TOKENS = 1024


def draw_dec_weight(key, part):
    key = jax.random.fold_in(key, 11)
    first, second, third = jax.random.split(key, 3)
    spread = math.log(10.0)
    base = jax.random.normal(first, (F, L, D), jnp.float32)
    rows = jnp.exp(jax.random.uniform(second, (F, L, 1), jnp.float32, -0.5 * spread, 0.5 * spread))
    columns = jnp.exp(jax.random.uniform(third, (1, 1, D), jnp.float32, -0.5 * spread, 0.5 * spread))
    layer_scale = 0.5 + jnp.arange(L, dtype=jnp.float32).reshape(1, L, 1) / (L - 1)
    values = base * rows * columns * layer_scale * (0.6 / math.sqrt(F))
    return jnp.clip(values, -2.0, 2.0).astype(jnp.bfloat16)


def levels(key, dims, cuts, least, largest):
    def one(axis_at, shards_of):
        heights = jax.random.uniform(jax.random.fold_in(jax.random.fold_in(key, 6), axis_at), (shards_of,), jnp.float32, least / len(cuts), largest / len(cuts))
        return jnp.repeat(jnp.exp(heights), dims[axis_at] // shards_of).reshape((-1,) + (1,) * (len(dims) - axis_at - 1))

    factor_of = one(*cuts[0])
    for cut in cuts[1:]:
        factor_of = factor_of * one(*cut)
    return factor_of


def centred(own_key, dims, scale, limit, cuts=(), kind=jnp.bfloat16):
    result = jax.random.normal(own_key, dims, jnp.float32) * scale
    if len(cuts) > 0:
        result = levels(own_key, dims, cuts, -0.22, 0.18) * result
    return jnp.clip(result, min=-limit, max=limit).astype(kind)


def setup_inputs(seed: int = 0) -> dict:
    key_of = jax.random.split(jax.random.key(seed), 6)
    acts = centred(key_of[0], (TOKENS, L, D), 1.0, 6.0, ((0, 16), (1, 8)))
    enc_weight = centred(key_of[1], (L, D, F), (L * D) ** -0.5, 0.046875, ((0, 8), (2, 16)))
    enc_bias = jnp.clip(-1.0 + 1.5 * jax.random.uniform(key_of[2], (F,), jnp.float32) ** levels(key_of[2], (F,), ((0, 16),), -0.2, 0.2), -1.0, 0.5)
    dec_weight = draw_dec_weight(jax.random.fold_in(key_of[5], 71), 0)
    dec_bias = centred(key_of[4], (L, D), 0.5, 3.0, ((0, 8),), jnp.float32)
    return {"acts": acts, "enc_weight": enc_weight, "enc_bias": enc_bias, "dec_weight": dec_weight, "dec_bias": dec_bias}


PENALTY = 0.05
EPS = 1e-06

def reference(acts, enc_weight, enc_bias, dec_weight, dec_bias):
    scale = 1.0 / math.sqrt(TOKENS)
    flat = acts.reshape(TOKENS, L * D)
    dec_flat = dec_weight.reshape(F, L * D)
    pre = jnp.dot(flat, enc_weight.reshape(L * D, F), preferred_element_type=jnp.float32) + enc_bias
    active = jnp.maximum(pre, 0.0)
    codes = (active * active).astype(jnp.bfloat16)
    norms = jnp.sqrt(lax.optimization_barrier(jnp.sum(jnp.square(dec_weight.astype(jnp.float32)), axis=2)) + EPS)
    totals = lax.optimization_barrier(jnp.sum(norms, axis=1))
    recon = jnp.dot(codes, dec_flat, preferred_element_type=jnp.float32) + dec_bias.reshape(1, L * D)
    recon_grad = (recon - flat.astype(jnp.float32)) * scale
    dec_bias_grad = lax.optimization_barrier(jnp.sum(recon_grad, axis=0)).reshape(L, D)
    recon_low = recon_grad.astype(jnp.bfloat16)
    code_grad = lax.dot_general(recon_low, dec_flat, (((1,), (1,)), ((), ())), preferred_element_type=jnp.float32)
    code_grad = code_grad + PENALTY * scale * totals
    pre_grad = code_grad * (2.0 * active)
    enc_bias_grad = lax.optimization_barrier(jnp.sum(pre_grad, axis=0))
    pre_low = pre_grad.astype(jnp.bfloat16)
    enc_grad = lax.dot_general(flat, pre_low, (((0,), (0,)), ((), ())), preferred_element_type=jnp.float32).reshape(L, D, F)
    code_sums = lax.optimization_barrier(jnp.sum(codes.astype(jnp.float32), axis=0))
    dec_grad = lax.dot_general(codes, recon_low, (((0,), (0,)), ((), ())), preferred_element_type=jnp.float32).reshape(F, L, D)
    dec_grad = dec_grad + PENALTY * scale * code_sums[:, None, None] * dec_weight.astype(jnp.float32) / norms[:, :, None]
    return (enc_grad, enc_bias_grad, dec_grad, dec_bias_grad)
```

```python
import functools
import math

import jax
import jax.numpy as jnp
from jax import lax
from jax.experimental import pallas as pl
from jax.experimental.pallas import tpu as pltpu
from jax.sharding import PartitionSpec as P

PENALTY = 0.05
EPS = 1e-06
MESH = pl.DeviceIdType.MESH
BF16 = jnp.bfloat16
F32 = jnp.float32

TOKENS = 1024
WIDTH = 2048
LATS = 1024
CHUNKS = 4
ROWS = TOKENS // CHUNKS
OWN = 16
SCALE = 1.0 / math.sqrt(TOKENS)
TILE = 256

STAGES = 18
SPAN = 4


def aligned(value, multiple):
    return pl.multiple_of(value, multiple)


CODE = 2.0**18
FLOOR = 2.0**-120


def pack(value):
    value = value * CODE
    return (value * value * (value * jnp.abs(value))).astype(BF16)


def unpack(coded):
    coded = coded.astype(F32)
    size = lax.rsqrt(lax.rsqrt(jnp.maximum(jnp.abs(coded), FLOOR))) * (1.0 / CODE)
    return jnp.where(coded < 0.0, -size, size)


def plain(value):
    return value.astype(BF16)


def widen(value):
    return value.astype(F32)


def step_kernel(
    acts, enc_hbm, enc_bias, dec_hbm, dec_bias,
    g_out, c_out, r_out, p_out, norm_out,
    enc, dec, gath, codes, low, plow,
    full1, full2, send1, send2, recv1, recv2, zsend1, zrecv1, zsend2, zrecv2, keep1, keep2, active,
    full3, send3, crecv, xsend, xrecv, zsend3, zrecv3, keep3, norm_row,
    ssem, rsem, lsem, osem,
):
    a = lax.axis_index("layer")
    b = lax.axis_index("latent")
    zl, y = a // 4, a % 4
    x, zh, c = b // 4, (b // 2) % 2, b % 2

    def ydev(d):
        return (zl * 4 + (y + d) % 4, b)

    zldev = ((1 - zl) * 4 + y, b)

    def xdev(d):
        return (a, ((x + d) % 4) * 4 + zh * 2 + c)

    zhdev = (a, x * 4 + (1 - zh) * 2 + c)
    cdev = (a, x * 4 + zh * 2 + 1 - c)

    load_enc = pltpu.make_async_copy(enc_hbm, enc, lsem.at[0])
    load_dec = pltpu.make_async_copy(dec_hbm, dec, lsem.at[1])
    load_enc.start()
    load_dec.start()

    barrier = pltpu.get_barrier_semaphore()
    peers = [zldev, zhdev, cdev] + [ydev(d) for d in (1, 2, 3)] + [xdev(d) for d in (1, 2, 3)]
    for peer in peers:
        pl.semaphore_signal(barrier, inc=1, device_id=peer, device_id_type=MESH)
    pl.semaphore_wait(barrier, len(peers))

    def push(stage, k, src, dst, device):
        pltpu.make_async_remote_copy(
            src_ref=src, dst_ref=dst, send_sem=ssem.at[stage, k], recv_sem=rsem.at[stage, k],
            device_id=device, device_id_type=MESH,
        ).start()

    def arrived(stage, k, ref):
        pltpu.make_async_copy(ref, ref, rsem.at[stage, k]).wait()

    def gone(stage, k, ref):
        pltpu.make_async_copy(ref, ref, ssem.at[stage, k]).wait()

    lat_slot = pl.ds(aligned(c * 128 + x * 32 + zh * 16, 16), 16)
    lat_zslot = pl.ds(aligned(c * 128 + x * 32 + (1 - zh) * 16, 16), 16)
    core_half = pl.ds(aligned(c * 128, 128), 128)
    lay_slot = pl.ds(aligned(y * 64 + zl * 32, 32), 32)
    lay_zslot = pl.ds(aligned(y * 64 + (1 - zl) * 32, 32), 32)

    def spread_lat(first, k, buf):
        ref = buf.at[k, lat_slot]
        push(first, k, ref, ref, zhdev)
        for d in (1, 2, 3):
            push(first + 1, k, ref, ref, xdev(d))

    def pass_lat(first, k, buf):
        ref = buf.at[k, lat_zslot]
        arrived(first, k, ref)
        for d in (1, 2, 3):
            push(first + 1, k, ref, ref, xdev(d))

    def pair_lat(first, k, buf):
        arrived(first + 1, k, buf.at[k, pl.ds(0, 96)])
        ref = buf.at[k, core_half]
        push(first + 2, k, ref, ref, cdev)

    def done_lat(first, k, buf):
        arrived(first + 2, k, buf.at[k, pl.ds(0, 128)])

    def spread_lay(first, k, buf):
        ref = buf.at[k, lay_slot]
        push(first, k, ref, ref, zldev)
        for d in (1, 2, 3):
            push(first + 1, k, ref, ref, ydev(d))

    def pass_lay(first, k, buf):
        ref = buf.at[k, lay_zslot]
        arrived(first, k, ref)
        for d in (1, 2, 3):
            push(first + 1, k, ref, ref, ydev(d))

    def done_lay(first, k, buf):
        arrived(first + 1, k, buf.at[k, pl.ds(0, 192)])

    def reduce_y(first, k, send, recv):
        for d in (1, 2, 3):
            rows = pl.ds(aligned(((y + d) % 4) * 64, 64), 64)
            push(first, k, send.at[k, rows], recv.at[k, d - 1], ydev(d))

    def reduce_z(first, k, full, recv, zsend, zrecv, keep, narrow, wide):
        arrived(first, k, recv.at[k])

        def total(half):
            value = full[k % 2, pl.ds(aligned(y * 64 + half * 32, 32), 32), :]
            for d in range(3):
                value = value + wide(recv[k, d, pl.ds(aligned(half * 32, 32), 32), :])
            return value

        zsend[k] = narrow(total(1 - zl))
        push(first + 1, k, zsend.at[k], zrecv.at[k], zldev)
        keep[k % 2] = total(zl)

    def m0(k):
        gath[k, lat_slot, :] = acts[pl.ds(aligned(k * OWN, OWN), OWN), :]
        spread_lat(0, k, gath)

    def m1(k):
        pass_lat(0, k, gath)

    def m2(k):
        pair_lat(0, k, gath)

    def m3(k):
        done_lat(0, k, gath)
        pltpu.make_async_copy(gath.at[k], g_out.at[k], osem.at[0]).start()

        def tile(n, _):
            cols = pl.ds(aligned(n * TILE, TILE), TILE)
            value = jnp.dot(gath[k], enc[:, cols], preferred_element_type=F32)
            full1[k % 2, :, cols] = value
            send1[k, :, cols] = pack(value)
            return 0

        lax.fori_loop(0, LATS // TILE, tile, 0)
        reduce_y(3, k, send1, recv1)

    def m4(k):
        reduce_z(3, k, full1, recv1, zsend1, zrecv1, keep1, pack, unpack)

    def m5(k):
        arrived(4, k, zrecv1.at[k])
        pre = keep1[k % 2] + unpack(zrecv1[k]) + enc_bias[...]
        value = jnp.maximum(pre, 0.0)
        active[k] = value
        codes[k, lay_slot, :] = (value * value).astype(BF16)
        spread_lay(5, k, codes)

    def m6(k):
        pass_lay(5, k, codes)

    def m7(k):
        done_lay(5, k, codes)
        pltpu.make_async_copy(codes.at[k], c_out.at[k], osem.at[1]).start()

        def tile(n, _):
            cols = pl.ds(aligned(n * TILE, TILE), TILE)
            value = jnp.dot(codes[k], dec[:, cols], preferred_element_type=F32)
            full3[k % 2, :, cols] = value
            send3[k, :, cols] = value.astype(BF16)
            return 0

        lax.fori_loop(0, WIDTH // TILE, tile, 0)
        other = pl.ds(aligned((1 - c) * 128, 128), 128)
        push(7, k, send3.at[k, other], crecv.at[k], cdev)

    def m8(k):
        arrived(7, k, crecv.at[k])
        for d in (1, 2, 3):
            to = (x + d) % 4
            value = full3[k % 2, pl.ds(aligned(c * 128 + to * 32, 32), 32), :]
            value = value + crecv[k, pl.ds(aligned(to * 32, 32), 32), :].astype(F32)
            xsend[k, d - 1] = value.astype(BF16)
            push(8, k, xsend.at[k, d - 1], xrecv.at[k, d - 1], xdev(d))

    def m9(k):
        arrived(8, k, xrecv.at[k])

        def total(half):
            value = full3[k % 2, pl.ds(aligned(c * 128 + x * 32 + half * 16, 16), 16), :]
            value = value + crecv[k, pl.ds(aligned(x * 32 + half * 16, 16), 16), :].astype(F32)
            for d in range(3):
                value = value + xrecv[k, d, pl.ds(aligned(half * 16, 16), 16), :].astype(F32)
            return value

        zsend3[k] = total(1 - zh).astype(BF16)
        push(9, k, zsend3.at[k], zrecv3.at[k], zhdev)
        keep3[k % 2] = total(zh)

    def m10(k):
        arrived(9, k, zrecv3.at[k])
        recon = keep3[k % 2] + zrecv3[k].astype(F32) + dec_bias[...]
        flat = acts[pl.ds(aligned(k * OWN, OWN), OWN), :].astype(F32)
        low[k, lat_slot, :] = ((recon - flat) * SCALE).astype(BF16)
        spread_lat(10, k, low)

    def m11(k):
        pass_lat(10, k, low)

    def m12(k):
        pair_lat(10, k, low)

    def m13(k):
        done_lat(10, k, low)
        pltpu.make_async_copy(low.at[k], r_out.at[k], osem.at[2]).start()

        def tile(n, _):
            cols = pl.ds(aligned(n * TILE, TILE), TILE)
            value = lax.dot_general(
                low[k], dec[cols, :], (((1,), (1,)), ((), ())), preferred_element_type=F32
            )
            value = value + (PENALTY * SCALE) * norm_row[0:1, cols]
            full2[k % 2, :, cols] = value
            send2[k, :, cols] = value.astype(BF16)
            return 0

        lax.fori_loop(0, LATS // TILE, tile, 0)
        reduce_y(13, k, send2, recv2)

    def m14(k):
        reduce_z(13, k, full2, recv2, zsend2, zrecv2, keep2, plain, widen)

    def m15(k):
        arrived(14, k, zrecv2.at[k])
        code_grad = keep2[k % 2] + zrecv2[k].astype(F32)
        plow[k, lay_slot, :] = (code_grad * (2.0 * active[k])).astype(BF16)
        spread_lay(15, k, plow)

    def m16(k):
        pass_lay(15, k, plow)

    def m17(k):
        done_lay(15, k, plow)
        pltpu.make_async_copy(plow.at[k], p_out.at[k], osem.at[3]).start()

    def norms():
        def tile(n, _):
            rows = pl.ds(aligned(n * 128, 128), 128)
            value = dec[rows, :].astype(F32)
            norm = jnp.sqrt(jnp.sum(value * value, axis=1, keepdims=True) + EPS)
            wide = jnp.broadcast_to(norm, (128, 128))
            norm_out[rows, :] = wide
            norm_row[:, rows] = wide.T[0:8, :]
            return 0

        lax.fori_loop(0, LATS // 128, tile, 0)

    stages = [m0, m1, m2, m3, m4, m5, m6, m7, m8, m9, m10, m11, m12, m13, m14, m15, m16, m17]

    def iteration(t, _):
        for place in range(SPAN):
            for m in reversed(range(place, STAGES, SPAN)):
                k = t - m // SPAN
                pl.when(jnp.logical_and(k >= 0, k < CHUNKS))(functools.partial(stages[m], k))
            if place == 0:

                @pl.when(t == 0)
                def _():
                    load_enc.wait()
                    load_dec.wait()
                    norms()

        return 0

    lax.fori_loop(0, CHUNKS + (STAGES - 1) // SPAN, iteration, 0)

    def drain(k, _):
        for first, buf in ((0, gath), (10, low)):
            gone(first, k, buf.at[k, pl.ds(0, 16)])
            gone(first + 1, k, buf.at[k, pl.ds(0, 96)])
            gone(first + 2, k, buf.at[k, pl.ds(0, 128)])
        for first, send in ((3, send1), (13, send2)):
            gone(first, k, send.at[k, pl.ds(0, 192)])
            gone(first + 1, k, send.at[k, pl.ds(0, 32)])
        for first, buf in ((5, codes), (15, plow)):
            gone(first, k, buf.at[k, pl.ds(0, 32)])
            gone(first + 1, k, buf.at[k, pl.ds(0, 192)])
        gone(7, k, crecv.at[k])
        gone(8, k, xsend.at[k])
        gone(9, k, zsend3.at[k])
        return 0

    lax.fori_loop(0, CHUNKS, drain, 0)
    pltpu.make_async_copy(gath, g_out, osem.at[0]).wait()
    pltpu.make_async_copy(codes, c_out, osem.at[1]).wait()
    pltpu.make_async_copy(low, r_out, osem.at[2]).wait()
    pltpu.make_async_copy(plow, p_out, osem.at[3]).wait()


def exchange(acts, enc, enc_bias, dec, dec_bias):
    any_spec = pl.BlockSpec(memory_space=pl.ANY)
    vmem = pl.BlockSpec(memory_space=pltpu.VMEM)
    V = pltpu.VMEM
    sums = [
        V((2, ROWS, LATS), F32), V((2, ROWS, LATS), F32),
        V((CHUNKS, ROWS, LATS), BF16), V((CHUNKS, ROWS, LATS), BF16),
        V((CHUNKS, 3, 64, LATS), BF16), V((CHUNKS, 3, 64, LATS), BF16),
        V((CHUNKS, 32, LATS), BF16), V((CHUNKS, 32, LATS), BF16),
        V((CHUNKS, 32, LATS), BF16), V((CHUNKS, 32, LATS), BF16),
        V((2, 32, LATS), F32), V((2, 32, LATS), F32), V((CHUNKS, 32, LATS), F32),
    ]
    recon = [
        V((2, ROWS, WIDTH), F32), V((CHUNKS, ROWS, WIDTH), BF16), V((CHUNKS, 128, WIDTH), BF16),
        V((CHUNKS, 3, 32, WIDTH), BF16), V((CHUNKS, 3, 32, WIDTH), BF16),
        V((CHUNKS, 16, WIDTH), BF16), V((CHUNKS, 16, WIDTH), BF16), V((2, 16, WIDTH), F32),
        V((8, LATS), F32),
    ]
    return pl.pallas_call(
        step_kernel,
        out_shape=[
            jax.ShapeDtypeStruct((CHUNKS, ROWS, WIDTH), BF16),
            jax.ShapeDtypeStruct((CHUNKS, ROWS, LATS), BF16),
            jax.ShapeDtypeStruct((CHUNKS, ROWS, WIDTH), BF16),
            jax.ShapeDtypeStruct((CHUNKS, ROWS, LATS), BF16),
            jax.ShapeDtypeStruct((LATS, 128), F32),
        ],
        in_specs=[vmem, any_spec, vmem, any_spec, vmem],
        out_specs=[any_spec, any_spec, any_spec, any_spec, vmem],
        scratch_shapes=[
            V((WIDTH, LATS), BF16), V((LATS, WIDTH), BF16),
            V((CHUNKS, ROWS, WIDTH), BF16), V((CHUNKS, ROWS, LATS), BF16),
            V((CHUNKS, ROWS, WIDTH), BF16), V((CHUNKS, ROWS, LATS), BF16),
            *sums, *recon,
            pltpu.SemaphoreType.DMA((STAGES, CHUNKS)),
            pltpu.SemaphoreType.DMA((STAGES, CHUNKS)),
            pltpu.SemaphoreType.DMA((2,)),
            pltpu.SemaphoreType.DMA((4,)),
        ],
        compiler_params=pltpu.CompilerParams(
            collective_id=0, has_side_effects=True, vmem_limit_bytes=60 << 20
        ),
        name="exchange",
    )(acts, enc, enc_bias, dec, dec_bias)


def rows_dot(left, right):
    return lax.dot_general(left, right, (((0,), (0,)), ((), ())), preferred_element_type=F32)


def enc_kernel(g, p, out, bias_out):
    out[...] = rows_dot(g[...], p[...])

    @pl.when(pl.program_id(0) == 0)
    def _():
        bias_out[...] = jnp.dot(jnp.ones((8, TOKENS), BF16), p[...], preferred_element_type=F32)


def enc_grads(g, p):
    n = 8
    w = WIDTH // n
    return pl.pallas_call(
        enc_kernel,
        grid=(n,),
        out_shape=[jax.ShapeDtypeStruct((WIDTH, LATS), F32), jax.ShapeDtypeStruct((8, LATS), F32)],
        in_specs=[
            pl.BlockSpec((TOKENS, w), lambda i: (0, i)),
            pl.BlockSpec((TOKENS, LATS), lambda i: (0, 0)),
        ],
        out_specs=[pl.BlockSpec((w, LATS), lambda i: (i, 0)), pl.BlockSpec((8, LATS), lambda i: (0, 0))],
        compiler_params=pltpu.CompilerParams(vmem_limit_bytes=56 << 20),
        name="enc_grads",
    )(g, p)


def dec_kernel(c, r, dec, norm, out, bias_out):
    sums = rows_dot(c[...], jnp.ones((TOKENS, 128), BF16))
    factor = (PENALTY * SCALE) * sums / norm[...]
    for i in range(4):
        cols = slice(i * 512, (i + 1) * 512)
        value = rows_dot(c[...], r[:, cols])
        for j in range(4):
            at = i * 4 + j
            part = value[:, j * 128 : (j + 1) * 128]
            part = part + factor * dec[:, at * 128 : (at + 1) * 128].astype(F32)
            out[pl.ds(at, part.shape[0], stride=16), :] = part

    @pl.when(pl.program_id(0) == 0)
    def _():
        bias_out[...] = jnp.dot(jnp.ones((8, TOKENS), BF16), r[...], preferred_element_type=F32)


def dec_grads(c, r, dec, norm):
    n = 4
    w = LATS // n
    return pl.pallas_call(
        dec_kernel,
        grid=(n,),
        out_shape=[jax.ShapeDtypeStruct((LATS * 16, 128), F32), jax.ShapeDtypeStruct((8, WIDTH), F32)],
        in_specs=[
            pl.BlockSpec((TOKENS, w), lambda i: (0, i)),
            pl.BlockSpec((TOKENS, WIDTH), lambda i: (0, 0)),
            pl.BlockSpec((w, WIDTH), lambda i: (i, 0)),
            pl.BlockSpec((w, 128), lambda i: (i, 0)),
        ],
        out_specs=[pl.BlockSpec((w * 16, 128), lambda i: (i, 0)), pl.BlockSpec((8, WIDTH), lambda i: (0, 0))],
        compiler_params=pltpu.CompilerParams(vmem_limit_bytes=56 << 20),
        name="dec_grads",
    )(c, r, dec, norm)


def on_device(acts, enc_weight, enc_bias, dec_weight, dec_bias):
    dec = dec_weight.reshape(LATS, WIDTH)
    g, c, r, p, norm = exchange(
        acts.reshape(TOKENS // 16, WIDTH), enc_weight.reshape(WIDTH, LATS), enc_bias.reshape(1, LATS), dec, dec_bias
    )
    g, r = g.reshape(TOKENS, WIDTH), r.reshape(TOKENS, WIDTH)
    c, p = c.reshape(TOKENS, LATS), p.reshape(TOKENS, LATS)
    dec_grad, dec_bias_grad = dec_grads(c, r, dec, norm)
    enc_grad, enc_bias_grad = enc_grads(g, p)
    return (
        enc_grad.reshape(1, WIDTH, LATS),
        enc_bias_grad[0],
        dec_grad.reshape(LATS, 1, WIDTH),
        dec_bias_grad[0:1],
    )


def solution(mesh):
    return jax.shard_map(
        on_device,
        mesh=mesh,
        in_specs=(
            P("latent", "layer", None),
            P("layer", None, "latent"),
            P("latent"),
            P("latent", "layer", None),
            P("layer", None),
        ),
        out_specs=(
            P("layer", None, "latent"),
            P("latent"),
            P("latent", "layer", None),
            P("layer", None),
        ),
        check_vma=False,
    )
```

```python
import functools
import math

import jax
import jax.numpy as jnp
from jax import lax
from jax.experimental import pallas as pl
from jax.experimental.pallas import tpu as pltpu
from jax.sharding import PartitionSpec as P

PENALTY = 0.05
EPS = 1e-06
MESH = pl.DeviceIdType.MESH
BF16 = jnp.bfloat16
F32 = jnp.float32

TOKENS = 1024
WIDTH = 2048
LATS = 1024
HALF = LATS // 2
PART = WIDTH // 2
CHUNKS = 8
ROWS = TOKENS // CHUNKS
SCALE = 1.0 / math.sqrt(TOKENS)
TILE = 512

STAGES = 18
SPAN = 1
SEMS = 25


def aligned(value, multiple):
    return pl.multiple_of(value, multiple)

CODE = 2.0**18
FLOOR = 2.0**-120


def pack(value):
    value = value * CODE
    return (value * value * (value * jnp.abs(value))).astype(BF16)


def unpack(coded):
    coded = coded.astype(F32)
    size = lax.rsqrt(lax.rsqrt(jnp.maximum(jnp.abs(coded), FLOOR))) * (1.0 / CODE)
    return jnp.where(coded < 0.0, -size, size)


def plain(value):
    return value.astype(BF16)


def widen(value):
    return value.astype(F32)


def step_kernel(
    acts, enc_hbm, enc_bias, dec_hbm, dec_bias,
    g_out, c_out, r_out, p_out, norm_out,
    enc, dec, dec_t, gath, codes, low, plow,
    sums1, sums2, active,
    full3, send3, crecv, xsend, xrecv, zsend3, zrecv3, keep3, norm_row,
    ssem, rsem, lsem, osem,
):
    a = lax.axis_index("layer")
    b = lax.axis_index("latent")
    zl, y = a // 4, a % 4
    x, zh, c = b // 4, (b // 2) % 2, b % 2

    def ydev(d):
        return (zl * 4 + (y + d) % 4, b)

    zldev = ((1 - zl) * 4 + y, b)

    def xdev(d):
        return (a, ((x + d) % 4) * 4 + zh * 2 + c)

    zhdev = (a, x * 4 + (1 - zh) * 2 + c)
    cdev = (a, x * 4 + zh * 2 + 1 - c)

    load_enc = pltpu.make_async_copy(enc_hbm, enc, lsem.at[0])
    load_dec = pltpu.make_async_copy(dec_hbm, dec, lsem.at[1])
    load_enc.start()
    load_dec.start()

    barrier = pltpu.get_barrier_semaphore()
    peers = [zldev, zhdev, cdev] + [ydev(d) for d in (1, 2, 3)] + [xdev(d) for d in (1, 2, 3)]
    for peer in peers:
        pl.semaphore_signal(barrier, inc=1, device_id=peer, device_id_type=MESH)
    pl.semaphore_wait(barrier, len(peers))

    def push(sem, k, src, dst, device):
        pltpu.make_async_remote_copy(
            src_ref=src, dst_ref=dst, send_sem=ssem.at[sem, k], recv_sem=rsem.at[sem, k],
            device_id=device, device_id_type=MESH,
        ).start()

    def arrived(sem, k, ref):
        pltpu.make_async_copy(ref, ref, rsem.at[sem, k]).wait()

    def gone(sem, k, ref):
        pltpu.make_async_copy(ref, ref, ssem.at[sem, k]).wait()

    left, right = pl.ds(0, HALF), pl.ds(HALF, HALF)
    mine = pl.ds(aligned(zh * PART, PART), PART)
    theirs = pl.ds(aligned((1 - zh) * PART, PART), PART)

    def sum_send(sem, k, bufs):
        send, ya, zb = bufs["send"], bufs["ya"], bufs["zb"]
        push(sem + 1, k, send.at[k, :, 1 - zl, :, right], zb.at[k], zldev)
        for d in (1, 2, 3):
            push(sem, k, send.at[k, (y + d) % 4, :, :, left], ya.at[k, d - 1], ydev(d))

    def sum_mid(sem, k, bufs, narrow, wide):
        full, ya, zb, za_send, za, mid, mid_f32, yb, keep = (
            bufs[n] for n in ("full", "ya", "zb", "za_send", "za", "mid", "mid_f32", "yb", "keep")
        )
        arrived(sem + 1, k, zb.at[k])
        value = full[k % 2, :, zl, :, right] + wide(zb[k])
        mid_f32[k % 2] = value
        mid[k] = narrow(value)
        for d in (1, 2, 3):
            push(sem + 3, k, mid.at[k, (y + d) % 4], yb.at[k, d - 1], ydev(d))
        arrived(sem, k, ya.at[k])

        def total(half):
            value = full[k % 2, y, half, :, left]
            for d in range(3):
                value = value + wide(ya[k, d, half])
            return value

        za_send[k] = narrow(total(1 - zl))
        push(sem + 2, k, za_send.at[k], za.at[k], zldev)
        keep[k % 2] = total(zl)

    def sum_end(sem, k, bufs, wide):
        za, mid_f32, yb, keep = (bufs[n] for n in ("za", "mid_f32", "yb", "keep"))
        arrived(sem + 3, k, yb.at[k])
        second = mid_f32[k % 2, y]
        for d in range(3):
            second = second + wide(yb[k, d])
        arrived(sem + 2, k, za.at[k])
        return keep[k % 2] + wide(za[k]), second

    def spread_send(sem, k, buf):
        first, second = buf.at[k, y, zl, :, left], buf.at[k, y, zl, :, right]
        push(sem, k, first, first, zldev)
        for d in (1, 2, 3):
            push(sem + 2, k, second, second, ydev(d))
            push(sem + 1, k, first, first, ydev(d))

    def spread_mid(sem, k, buf):
        first = buf.at[k, y, 1 - zl, :, left]
        arrived(sem, k, first)
        for d in (1, 2, 3):
            push(sem + 1, k, first, first, ydev(d))
        arrived(sem + 2, k, buf.at[k, pl.ds(0, 3), 0, :, right])
        column = buf.at[k, :, zl, :, right]
        push(sem + 3, k, column, column, zldev)

    def spread_end(sem, k, buf):
        arrived(sem + 1, k, buf.at[k, pl.ds(0, 3), :, :, left])
        arrived(sem + 3, k, buf.at[k, :, 0, :, right])

    def even(stage):
        def run(k):
            pl.when(k % 2 == 0)(functools.partial(stage, k))

        return run

    def m0(k):
        gath[k + zh, c, x] = acts[pl.ds(aligned(k * 8, 16), 16), :]
        ref = gath.at[k + zh, c, x]
        push(0, k, ref, ref, zhdev)
        for d in (1, 2, 3):
            push(1, k, ref, ref, xdev(d))

    def m1(k):
        ref = gath.at[k + 1 - zh, c, x]
        arrived(0, k, ref)
        for d in (1, 2, 3):
            push(1, k, ref, ref, xdev(d))

    def m2(k):
        arrived(1, k, gath.at[pl.ds(k, 2), 0, pl.ds(0, 3)])
        ref = gath.at[pl.ds(k, 2), c]
        push(2, k, ref, ref, cdev)

    def wait_pair(k):
        arrived(2, k, gath.at[pl.ds(k, 2), 1 - c])

    def m3(k):
        even(wait_pair)(k)
        pltpu.make_async_copy(gath.at[k], g_out.at[k], osem.at[0]).start()

        def tile(n, _):
            cols = pl.ds(aligned(n * TILE, TILE), TILE)
            left_rows = gath[k].reshape(ROWS, WIDTH)
            value = jnp.dot(left_rows, enc[:, cols], preferred_element_type=F32).reshape(4, 2, 16, TILE)
            sums1["full"][k % 2, :, :, :, cols] = value
            sums1["send"][k, :, :, :, cols] = pack(value)
            return 0

        lax.fori_loop(0, LATS // TILE, tile, 0)
        sum_send(3, k, sums1)

    def m4(k):
        sum_mid(3, k, sums1, pack, unpack)

    def m5(k):
        for value, cols in zip(sum_end(3, k, sums1, unpack), (left, right)):
            value = jnp.maximum(value + enc_bias[:, cols], 0.0)
            active[k, :, cols] = value
            codes[k, y, zl, :, cols] = (value * value).astype(BF16)
        spread_send(7, k, codes)

    def m6(k):
        spread_mid(7, k, codes)

    def m7(k):
        spread_end(7, k, codes)
        pltpu.make_async_copy(codes.at[k], c_out.at[k], osem.at[1]).start()

        def tile(n, _):
            cols = pl.ds(aligned(n * TILE, TILE), TILE)
            rows = codes[k].reshape(ROWS, LATS)
            value = jnp.dot(rows, dec[:, cols], preferred_element_type=F32).reshape(2, 4, 16, TILE)
            full3[k % 2, :, :, :, cols] = value
            send3[k, :, :, :, cols] = value.astype(BF16)
            return 0

        lax.fori_loop(0, WIDTH // TILE, tile, 0)
        push(11, k, send3.at[k, 1 - c], crecv.at[k], cdev)

    def m8(k):
        arrived(11, k, crecv.at[k])
        for d in (1, 2, 3):
            to = (x + d) % 4
            xsend[k, d - 1] = (full3[k % 2, c, to] + crecv[k, to].astype(F32)).astype(BF16)
            push(12, k, xsend.at[k, d - 1], xrecv.at[k, d - 1], xdev(d))

    def m9(k):
        arrived(12, k, xrecv.at[k])

        def total(cols):
            value = full3[k % 2, c, x, :, cols] + crecv[k, x, :, cols].astype(F32)
            for d in range(3):
                value = value + xrecv[k, d, :, cols].astype(F32)
            return value

        zsend3[k] = total(theirs).astype(BF16)
        push(13, k, zsend3.at[k], zrecv3.at[k], zhdev)
        keep3[k % 2] = total(mine)

    def m10(k):
        arrived(13, k, zrecv3.at[k])
        recon = keep3[k % 2] + zrecv3[k].astype(F32) + dec_bias[:, mine]
        flat = gath[k, c, x, :, mine].astype(F32)
        low[k, c, x, :, mine] = ((recon - flat) * SCALE).astype(BF16)
        ref = low.at[k, c, x, :, mine]
        push(14, k, ref, ref, zhdev)
        for d in (1, 2, 3):
            push(15, k, ref, ref, xdev(d))

    def m11(k):
        ref = low.at[k, c, x, :, theirs]
        arrived(14, k, ref)
        for d in (1, 2, 3):
            push(15, k, ref, ref, xdev(d))

    def m12(k):
        arrived(15, k, low.at[k, 0, pl.ds(0, 3)])
        ref = low.at[k, c]
        push(16, k, ref, ref, cdev)

    def m13(k):
        arrived(16, k, low.at[k, 1 - c])
        pltpu.make_async_copy(low.at[k], r_out.at[k], osem.at[2]).start()

        def tile(n, _):
            cols = pl.ds(aligned(n * TILE, TILE), TILE)
            rows = low[k].reshape(ROWS, WIDTH)
            value = jnp.dot(rows, dec_t[:, cols], preferred_element_type=F32)
            value = (value + (PENALTY * SCALE) * norm_row[0:1, cols]).reshape(4, 2, 16, TILE)
            sums2["full"][k % 2, :, :, :, cols] = value
            sums2["send"][k, :, :, :, cols] = value.astype(BF16)
            return 0

        lax.fori_loop(0, LATS // TILE, tile, 0)
        sum_send(17, k, sums2)

    def m14(k):
        sum_mid(17, k, sums2, plain, widen)

    def m15(k):
        for value, cols in zip(sum_end(17, k, sums2, widen), (left, right)):
            plow[k, y, zl, :, cols] = (value * (2.0 * active[k, :, cols])).astype(BF16)
        spread_send(21, k, plow)

    def m16(k):
        spread_mid(21, k, plow)

    def m17(k):
        spread_end(21, k, plow)
        pltpu.make_async_copy(plow.at[k], p_out.at[k], osem.at[3]).start()

    def prepare(n):
        rows = pl.ds(aligned(n * 128, 128), 128)
        block = dec[rows, :]
        value = block.astype(F32)
        norm = jnp.sqrt(jnp.sum(value * value, axis=1, keepdims=True) + EPS)
        wide = jnp.broadcast_to(norm, (128, 128))
        norm_out[rows, :] = wide
        norm_row[:, rows] = wide.T[0:8, :]
        dec_t[:, rows] = block.T

    stages = [even(m0), even(m1), even(m2), m3, m4, m5, m6, m7, m8, m9, m10, m11, m12, m13, m14, m15, m16, m17]

    def iteration(t, _):
        for place in range(SPAN):
            for m in reversed(range(place, STAGES, SPAN)):
                k = t - m // SPAN
                pl.when(jnp.logical_and(k >= 0, k < CHUNKS))(functools.partial(stages[m], k))
            if place == 0:

                @pl.when(t == 0)
                def _():
                    load_enc.wait()
                    load_dec.wait()

                @pl.when(t < 4)
                def _():
                    prepare(2 * t)
                    prepare(2 * t + 1)

        return 0

    lax.fori_loop(0, CHUNKS + (STAGES - 1) // SPAN, iteration, 0)

    def drain(k, _):
        @pl.when(k % 2 == 0)
        def _():
            gone(0, k, gath.at[k, 0, 0])
            gone(1, k, gath.at[pl.ds(k, 2), 0, pl.ds(0, 3)])
            gone(2, k, gath.at[pl.ds(k, 2), 0])

        for sem, bufs in ((3, sums1), (17, sums2)):
            gone(sem, k, bufs["ya"].at[k])
            gone(sem + 1, k, bufs["zb"].at[k])
            gone(sem + 2, k, bufs["za"].at[k])
            gone(sem + 3, k, bufs["yb"].at[k])
        for sem, buf in ((7, codes), (21, plow)):
            gone(sem, k, buf.at[k, 0, 0, :, left])
            gone(sem + 1, k, buf.at[k, pl.ds(0, 3), :, :, left])
            gone(sem + 2, k, buf.at[k, pl.ds(0, 3), 0, :, left])
            gone(sem + 3, k, buf.at[k, :, 0, :, left])
        gone(11, k, crecv.at[k])
        gone(12, k, xsend.at[k])
        gone(13, k, zsend3.at[k])
        gone(14, k, zsend3.at[k])
        gone(15, k, low.at[k, 0, pl.ds(0, 3)])
        gone(16, k, low.at[k, 0])
        return 0

    lax.fori_loop(0, CHUNKS, drain, 0)
    pltpu.make_async_copy(gath, g_out, osem.at[0]).wait()
    pltpu.make_async_copy(codes, c_out, osem.at[1]).wait()
    pltpu.make_async_copy(low, r_out, osem.at[2]).wait()
    pltpu.make_async_copy(plow, p_out, osem.at[3]).wait()


def layer_sum():
    V = pltpu.VMEM
    return {
        "full": V((2, 4, 2, 16, LATS), F32),
        "send": V((CHUNKS, 4, 2, 16, LATS), BF16),
        "ya": V((CHUNKS, 3, 2, 16, HALF), BF16),
        "zb": V((CHUNKS, 4, 16, HALF), BF16),
        "za_send": V((CHUNKS, 16, HALF), BF16),
        "za": V((CHUNKS, 16, HALF), BF16),
        "mid": V((CHUNKS, 4, 16, HALF), BF16),
        "mid_f32": V((2, 4, 16, HALF), F32),
        "yb": V((CHUNKS, 3, 16, HALF), BF16),
        "keep": V((2, 16, HALF), F32),
    }


def exchange(acts, enc, enc_bias, dec, dec_bias):
    any_spec = pl.BlockSpec(memory_space=pl.ANY)
    vmem = pl.BlockSpec(memory_space=pltpu.VMEM)
    V = pltpu.VMEM
    by_latent = (CHUNKS, 2, 4, 16, WIDTH)
    by_layer = (CHUNKS, 4, 2, 16, LATS)
    return pl.pallas_call(
        step_kernel,
        out_shape=[
            jax.ShapeDtypeStruct(by_latent, BF16),
            jax.ShapeDtypeStruct(by_layer, BF16),
            jax.ShapeDtypeStruct(by_latent, BF16),
            jax.ShapeDtypeStruct(by_layer, BF16),
            jax.ShapeDtypeStruct((LATS, 128), F32),
        ],
        in_specs=[vmem, any_spec, vmem, any_spec, vmem],
        out_specs=[any_spec, any_spec, any_spec, any_spec, vmem],
        scratch_shapes=[
            V((WIDTH, LATS), BF16), V((LATS, WIDTH), BF16), V((WIDTH, LATS), BF16),
            V(by_latent, BF16), V(by_layer, BF16), V(by_latent, BF16), V(by_layer, BF16),
            layer_sum(), layer_sum(), V((CHUNKS, 16, LATS), F32),
            V((2, 2, 4, 16, WIDTH), F32), V(by_latent, BF16), V((CHUNKS, 4, 16, WIDTH), BF16),
            V((CHUNKS, 3, 16, WIDTH), BF16), V((CHUNKS, 3, 16, WIDTH), BF16),
            V((CHUNKS, 16, PART), BF16), V((CHUNKS, 16, PART), BF16), V((2, 16, PART), F32),
            V((8, LATS), F32),
            pltpu.SemaphoreType.DMA((SEMS, CHUNKS)),
            pltpu.SemaphoreType.DMA((SEMS, CHUNKS)),
            pltpu.SemaphoreType.DMA((2,)),
            pltpu.SemaphoreType.DMA((4,)),
        ],
        compiler_params=pltpu.CompilerParams(
            collective_id=0, has_side_effects=True, vmem_limit_bytes=60 << 20
        ),
        name="exchange",
    )(acts, enc, enc_bias, dec, dec_bias)


def rows_dot(left, right):
    return lax.dot_general(left, right, (((0,), (0,)), ((), ())), preferred_element_type=F32)


def enc_kernel(g, p, out, bias_out):
    out[...] = rows_dot(g[...], p[...])

    @pl.when(pl.program_id(0) == 0)
    def _():
        bias_out[...] = jnp.dot(jnp.ones((8, TOKENS), BF16), p[...], preferred_element_type=F32)


def enc_grads(g, p):
    n = 8
    w = WIDTH // n
    return pl.pallas_call(
        enc_kernel,
        grid=(n,),
        out_shape=[jax.ShapeDtypeStruct((WIDTH, LATS), F32), jax.ShapeDtypeStruct((8, LATS), F32)],
        in_specs=[
            pl.BlockSpec((TOKENS, w), lambda i: (0, i)),
            pl.BlockSpec((TOKENS, LATS), lambda i: (0, 0)),
        ],
        out_specs=[pl.BlockSpec((w, LATS), lambda i: (i, 0)), pl.BlockSpec((8, LATS), lambda i: (0, 0))],
        compiler_params=pltpu.CompilerParams(vmem_limit_bytes=56 << 20),
        name="enc_grads",
    )(g, p)


def dec_kernel(c, r, dec, norm, out, bias_out):
    sums = rows_dot(c[...], jnp.ones((TOKENS, 128), BF16))
    factor = (PENALTY * SCALE) * sums / norm[...]
    for i in range(4):
        cols = slice(i * 512, (i + 1) * 512)
        value = rows_dot(c[...], r[:, cols])
        for j in range(4):
            at = i * 4 + j
            part = value[:, j * 128 : (j + 1) * 128]
            part = part + factor * dec[:, at * 128 : (at + 1) * 128].astype(F32)
            out[pl.ds(at, part.shape[0], stride=16), :] = part

    @pl.when(pl.program_id(0) == 0)
    def _():
        bias_out[...] = jnp.dot(jnp.ones((8, TOKENS), BF16), r[...], preferred_element_type=F32)


def dec_grads(c, r, dec, norm):
    n = 4
    w = LATS // n
    return pl.pallas_call(
        dec_kernel,
        grid=(n,),
        out_shape=[jax.ShapeDtypeStruct((LATS * 16, 128), F32), jax.ShapeDtypeStruct((8, WIDTH), F32)],
        in_specs=[
            pl.BlockSpec((TOKENS, w), lambda i: (0, i)),
            pl.BlockSpec((TOKENS, WIDTH), lambda i: (0, 0)),
            pl.BlockSpec((w, WIDTH), lambda i: (i, 0)),
            pl.BlockSpec((w, 128), lambda i: (i, 0)),
        ],
        out_specs=[pl.BlockSpec((w * 16, 128), lambda i: (i, 0)), pl.BlockSpec((8, WIDTH), lambda i: (0, 0))],
        compiler_params=pltpu.CompilerParams(vmem_limit_bytes=56 << 20),
        name="dec_grads",
    )(c, r, dec, norm)


def on_device(acts, enc_weight, enc_bias, dec_weight, dec_bias):
    dec = dec_weight.reshape(LATS, WIDTH)
    g, c, r, p, norm = exchange(
        acts.reshape(TOKENS // 16, WIDTH), enc_weight.reshape(WIDTH, LATS), enc_bias.reshape(1, LATS), dec, dec_bias
    )
    g, r = g.reshape(TOKENS, WIDTH), r.reshape(TOKENS, WIDTH)
    c, p = c.reshape(TOKENS, LATS), p.reshape(TOKENS, LATS)
    dec_grad, dec_bias_grad = dec_grads(c, r, dec, norm)
    enc_grad, enc_bias_grad = enc_grads(g, p)
    return (
        enc_grad.reshape(1, WIDTH, LATS),
        enc_bias_grad[0],
        dec_grad.reshape(LATS, 1, WIDTH),
        dec_bias_grad[0:1],
    )


def solution(mesh):
    return jax.shard_map(
        on_device,
        mesh=mesh,
        in_specs=(
            P("latent", "layer", None),
            P("layer", None, "latent"),
            P("latent"),
            P("latent", "layer", None),
            P("layer", None),
        ),
        out_specs=(
            P("layer", None, "latent"),
            P("latent"),
            P("latent", "layer", None),
            P("layer", None),
        ),
        check_vma=False,
    )
```

```python
import functools
import math

import jax
import jax.numpy as jnp
from jax import lax
from jax.experimental import pallas as pl
from jax.experimental.pallas import tpu as pltpu
from jax.sharding import PartitionSpec as P

PENALTY = 0.05
EPS = 1e-06
MESH = pl.DeviceIdType.MESH
BF16 = jnp.bfloat16
F32 = jnp.float32

TOKENS = 1024
WIDTH = 2048
LATS = 1024
HALF = LATS // 2
PART = WIDTH // 2
CHUNKS = 8
ROWS = TOKENS // CHUNKS
SCALE = 1.0 / math.sqrt(TOKENS)
TILE = 512

SEMS = 25

HOPS = (1.0,) * 17
STARTS = tuple(sum(HOPS[:m]) for m in range(len(HOPS) + 1))
LAGS = tuple(int(start) for start in STARTS)
ORDER = tuple(sorted(range(len(STARTS)), key=lambda m: (STARTS[m] % 1.0, -m)))


def before(first, second, ahead):
    at = (LAGS[first], ORDER.index(first))
    return at < (LAGS[second] + ahead, ORDER.index(second))


FULL = CHUNKS - 1 + LAGS[13]
assert FULL + 4 <= CHUNKS + LAGS[-1]
assert all(before(m, m + 1, 0) for m in range(len(HOPS)))
assert all(before(last, first, 2) for first, last in ((3, 4), (4, 5), (7, 9), (9, 10), (13, 14), (14, 15)))


def aligned(value, multiple):
    return pl.multiple_of(value, multiple)

CODE = 2.0**18
FLOOR = 2.0**-120


def pack(value):
    value = value * CODE
    return (value * value * (value * jnp.abs(value))).astype(BF16)


def unpack(coded):
    coded = coded.astype(F32)
    size = lax.rsqrt(lax.rsqrt(jnp.maximum(jnp.abs(coded), FLOOR))) * (1.0 / CODE)
    return jnp.where(coded < 0.0, -size, size)


def plain(value):
    return value.astype(BF16)


def widen(value):
    return value.astype(F32)


def step_kernel(
    acts, enc_hbm, enc_bias, dec_hbm, dec_bias,
    g_out, p_out, d_out, low_sum, plow_sum,
    enc, dec, dec_t, gath, codes, low, plow,
    sums1, sums2, active,
    full3, send3, crecv, xsend, xrecv, zsend3, zrecv3, keep3, norm_row, norm_wide, factor, code_sum, products,
    ssem, rsem, lsem, osem,
):
    a = lax.axis_index("layer")
    b = lax.axis_index("latent")
    zl, y = a // 4, a % 4
    x, zh, c = b // 4, (b // 2) % 2, b % 2

    def ydev(d):
        return (zl * 4 + (y + d) % 4, b)

    zldev = ((1 - zl) * 4 + y, b)

    def xdev(d):
        return (a, ((x + d) % 4) * 4 + zh * 2 + c)

    zhdev = (a, x * 4 + (1 - zh) * 2 + c)
    cdev = (a, x * 4 + zh * 2 + 1 - c)

    load_enc = pltpu.make_async_copy(enc_hbm, enc, lsem.at[0])
    load_dec = pltpu.make_async_copy(dec_hbm, dec, lsem.at[1])
    load_enc.start()
    load_dec.start()

    barrier = pltpu.get_barrier_semaphore()
    peers = [zldev, zhdev, cdev] + [ydev(d) for d in (1, 2, 3)] + [xdev(d) for d in (1, 2, 3)]
    for peer in peers:
        pl.semaphore_signal(barrier, inc=1, device_id=peer, device_id_type=MESH)
    pl.semaphore_wait(barrier, len(peers))

    def push(sem, k, src, dst, device):
        pltpu.make_async_remote_copy(
            src_ref=src, dst_ref=dst, send_sem=ssem.at[sem, k], recv_sem=rsem.at[sem, k],
            device_id=device, device_id_type=MESH,
        ).start()

    def arrived(sem, k, ref):
        pltpu.make_async_copy(ref, ref, rsem.at[sem, k]).wait()

    def gone(sem, k, ref):
        pltpu.make_async_copy(ref, ref, ssem.at[sem, k]).wait()

    left, right = pl.ds(0, HALF), pl.ds(HALF, HALF)
    lower, upper = pl.ds(0, PART), pl.ds(PART, PART)
    mine = pl.ds(aligned(zh * PART, PART), PART)
    theirs = pl.ds(aligned((1 - zh) * PART, PART), PART)

    def sum_send(sem, k, bufs):
        send, ya, zb = bufs["send"], bufs["ya"], bufs["zb"]
        push(sem + 1, k, send.at[k, :, 1 - zl, :, right], zb.at[k], zldev)
        for d in (1, 2, 3):
            push(sem, k, send.at[k, (y + d) % 4, :, :, left], ya.at[k, d - 1], ydev(d))

    def sum_mid(sem, k, bufs, narrow, wide):
        full, ya, zb, za_send, za, mid, mid_f32, yb, keep = (
            bufs[n] for n in ("full", "ya", "zb", "za_send", "za", "mid", "mid_f32", "yb", "keep")
        )
        arrived(sem + 1, k, zb.at[k])
        value = full[k % 2, :, zl, :, right] + wide(zb[k])
        mid_f32[k % 2] = value
        mid[k] = narrow(value)
        for d in (1, 2, 3):
            push(sem + 3, k, mid.at[k, (y + d) % 4], yb.at[k, d - 1], ydev(d))
        arrived(sem, k, ya.at[k])

        def total(half):
            value = full[k % 2, y, half, :, left]
            for d in range(3):
                value = value + wide(ya[k, d, half])
            return value

        za_send[k] = narrow(total(1 - zl))
        push(sem + 2, k, za_send.at[k], za.at[k], zldev)
        keep[k % 2] = total(zl)

    def sum_end(sem, k, bufs, wide):
        za, mid_f32, yb, keep = (bufs[n] for n in ("za", "mid_f32", "yb", "keep"))
        arrived(sem + 3, k, yb.at[k])
        second = mid_f32[k % 2, y]
        for d in range(3):
            second = second + wide(yb[k, d])
        arrived(sem + 2, k, za.at[k])
        return keep[k % 2] + wide(za[k]), second

    def spread_send(sem, k, buf):
        own, first = buf.at[k, y, zl], buf.at[k, y, zl, :, left]
        push(sem, k, first, first, zldev)
        for d in (1, 2, 3):
            push(sem + 2, k, own, own, ydev(d))

    def spread_mid(sem, k, buf):
        first = buf.at[k, y, 1 - zl, :, left]
        arrived(sem, k, first)
        for d in (1, 2, 3):
            push(sem + 1, k, first, first, ydev(d))
        arrived(sem + 2, k, buf.at[k, pl.ds(0, 3), 0])
        column = buf.at[k, :, zl, :, right]
        push(sem + 3, k, column, column, zldev)

    def spread_end(sem, k, buf):
        arrived(sem + 1, k, buf.at[k, pl.ds(0, 3), 0, :, left])
        arrived(sem + 3, k, buf.at[k, :, 0, :, right])

    def m0(pair):
        k = 2 * pair
        gath[k + zh, c, x] = acts[pl.ds(aligned(k * 8, 16), 16), :]
        ref = gath.at[k + zh, c, x]
        push(0, k, ref, ref, zhdev)
        for d in (1, 2, 3):
            push(1, k, ref, ref, xdev(d))

    def m1(pair):
        k = 2 * pair
        ref = gath.at[k + 1 - zh, c, x]
        arrived(0, k, ref)
        for d in (1, 2, 3):
            push(1, k, ref, ref, xdev(d))

    def m2(pair):
        k = 2 * pair
        arrived(1, k, gath.at[pl.ds(k, 2), 0, pl.ds(0, 3)])
        ref = gath.at[pl.ds(k, 2), c]
        push(2, k, ref, ref, cdev)

    def wait_pair(k):
        arrived(2, k, gath.at[pl.ds(k, 2), 1 - c])

    def m3(k):
        pl.when(k % 2 == 0)(functools.partial(wait_pair, k))
        pltpu.make_async_copy(gath.at[k], g_out.at[k], osem.at[0]).start()

        def tile(n, _):
            cols = pl.ds(aligned(n * TILE, TILE), TILE)
            left_rows = gath[k].reshape(ROWS, WIDTH)
            value = jnp.dot(left_rows, enc[:, cols], preferred_element_type=F32).reshape(4, 2, 16, TILE)
            sums1["full"][k % 2, :, :, :, cols] = value
            sums1["send"][k, :, :, :, cols] = pack(value)
            return 0

        lax.fori_loop(0, LATS // TILE, tile, 0)
        sum_send(3, k, sums1)

    def m4(k):
        sum_mid(3, k, sums1, pack, unpack)

    def m5(k):
        for value, cols in zip(sum_end(3, k, sums1, unpack), (left, right)):
            value = jnp.maximum(value + enc_bias[:, cols], 0.0)
            active[k, :, cols] = value
            codes[k, y, zl, :, cols] = (value * value).astype(BF16)
        spread_send(7, k, codes)

    def m6(k):
        spread_mid(7, k, codes)

    def add_rows(total, k, rows):
        part = jnp.sum(rows.astype(F32).reshape(ROWS // 8, 8, rows.shape[1]), axis=0)
        total[...] = jnp.where(k == 0, part, total[...] + part)

    def m7(k):
        spread_end(7, k, codes)

        def tile(n, _):
            cols = pl.ds(aligned(n * TILE, TILE), TILE)
            rows = codes[k].reshape(ROWS, LATS)
            value = jnp.dot(rows, dec[:, cols], preferred_element_type=F32).reshape(2, 4, 16, TILE)
            full3[k % 2, :, :, :, cols] = value
            send3[k, :, :, :, cols] = value.astype(BF16)
            return 0

        lax.fori_loop(0, WIDTH // TILE, tile, 0)
        push(11, k, send3.at[k, 1 - c], crecv.at[k], cdev)
        add_rows(code_sum, k, codes[k].reshape(ROWS, LATS))

        @pl.when(k == CHUNKS - 1)
        def _():
            total = jnp.sum(code_sum[...], axis=0, keepdims=True) * (PENALTY * SCALE)
            factor[...] = jnp.broadcast_to(total, (128, LATS)).T / norm_wide[...]

    def m8(k):
        arrived(11, k, crecv.at[k])
        for d in (1, 2, 3):
            to = (x + d) % 4
            xsend[k, d - 1] = (full3[k % 2, c, to] + crecv[k, to].astype(F32)).astype(BF16)
            push(12, k, xsend.at[k, d - 1], xrecv.at[k, d - 1], xdev(d))

    def m9(k):
        arrived(12, k, xrecv.at[k])

        def total(cols):
            value = full3[k % 2, c, x, :, cols] + crecv[k, x, :, cols].astype(F32)
            for d in range(3):
                value = value + xrecv[k, d, :, cols].astype(F32)
            return value

        zsend3[k] = total(theirs).astype(BF16)
        push(13, k, zsend3.at[k], zrecv3.at[k], zhdev)
        keep3[k % 2] = total(mine)

    def m10(k):
        arrived(13, k, zrecv3.at[k])
        recon = keep3[k % 2] + zrecv3[k].astype(F32) + dec_bias[:, mine]
        flat = gath[k, c, x, :, mine].astype(F32)
        low[k, c, x, :, mine] = ((recon - flat) * SCALE).astype(BF16)
        ref = low.at[k, c, x, :, mine]
        push(14, k, ref, ref, zhdev)
        for d in (1, 2, 3):
            push(15, k, ref, ref, xdev(d))

    def m11(k):
        ref = low.at[k, c, x, :, theirs]
        arrived(14, k, ref)
        for d in (1, 2, 3):
            push(15, k, ref, ref, xdev(d))

    def m12(k):
        arrived(15, k, low.at[k, 0, pl.ds(0, 3)])
        ref = low.at[k, c]
        push(16, k, ref, ref, cdev)

    def m13(k):
        arrived(16, k, low.at[k, 1 - c])

        def tile(n, _):
            cols = pl.ds(aligned(n * TILE, TILE), TILE)
            rows = low[k].reshape(ROWS, WIDTH)
            value = jnp.dot(rows, dec_t[:, cols], preferred_element_type=F32)
            value = (value + (PENALTY * SCALE) * norm_row[0:1, cols]).reshape(4, 2, 16, TILE)
            sums2["full"][k % 2, :, :, :, cols] = value
            sums2["send"][k, :, :, :, cols] = value.astype(BF16)
            return 0

        lax.fori_loop(0, LATS // TILE, tile, 0)
        sum_send(17, k, sums2)
        add_rows(low_sum, k, low[k].reshape(ROWS, WIDTH))

    def m14(k):
        sum_mid(17, k, sums2, plain, widen)

    def m15(k):
        for value, cols in zip(sum_end(17, k, sums2, widen), (left, right)):
            plow[k, y, zl, :, cols] = (value * (2.0 * active[k, :, cols])).astype(BF16)
        spread_send(21, k, plow)

    def m16(k):
        spread_mid(21, k, plow)

    def m17(k):
        spread_end(21, k, plow)
        pltpu.make_async_copy(plow.at[k], p_out.at[k], osem.at[1]).start()
        add_rows(plow_sum, k, plow[k].reshape(ROWS, LATS))

    def prepare(n):
        rows = pl.ds(aligned(n * 128, 128), 128)
        block = dec[rows, :]
        value = block.astype(F32)
        norm = jnp.sqrt(jnp.sum(value * value, axis=1, keepdims=True) + EPS)
        wide = jnp.broadcast_to(norm, (128, 128))
        norm_wide[rows, :] = wide
        norm_row[:, rows] = wide.T[0:8, :]
        dec_t[:, rows] = block.T

    def decoder_product(n):
        rows = pl.ds(aligned(n * (LATS // 4), LATS // 4), LATS // 4)
        left_side = codes[:, :, :, :, rows].reshape(TOKENS, LATS // 4)
        for half in (lower, upper):
            right_side = low[:, :, :, :, half].reshape(TOKENS, PART)
            value = rows_dot(left_side, right_side)
            penalty = jnp.tile(factor[rows, :], (1, PART // 128)) * dec[rows, half].astype(F32)
            products[rows, half] = (value + penalty).astype(BF16)
        pltpu.make_async_copy(products.at[rows], d_out.at[rows], osem.at[2]).start()

    stages = [m0, m1, m2, m3, m4, m5, m6, m7, m8, m9, m10, m11, m12, m13, m14, m15, m16, m17]

    def iteration(t, _):
        for m in ORDER:
            k = t - LAGS[m]
            if m == 3:
                pl.when(k == 0)(load_enc.wait)
            ready = jnp.logical_and(k >= 0, k < CHUNKS)
            if m < 3:
                ready = jnp.logical_and(ready, k % 2 == 0)
            pl.when(ready)(functools.partial(stages[m], k // 2 if m < 3 else k))
        @pl.when(jnp.logical_and(t >= FULL, t < FULL + 4))
        def _():
            decoder_product(t - FULL)

        pl.when(t == 0)(load_dec.wait)

        @pl.when(t < 4)
        def _():
            prepare(2 * t)
            prepare(2 * t + 1)

        return 0

    lax.fori_loop(0, CHUNKS + LAGS[-1], iteration, 0)

    def drain(k, _):
        @pl.when(k % 2 == 0)
        def _():
            gone(0, k, gath.at[k, 0, 0])
            gone(1, k, gath.at[pl.ds(k, 2), 0, pl.ds(0, 3)])
            gone(2, k, gath.at[pl.ds(k, 2), 0])

        for sem, bufs in ((3, sums1), (17, sums2)):
            gone(sem, k, bufs["ya"].at[k])
            gone(sem + 1, k, bufs["zb"].at[k])
            gone(sem + 2, k, bufs["za"].at[k])
            gone(sem + 3, k, bufs["yb"].at[k])
        for sem, buf in ((7, codes), (21, plow)):
            gone(sem, k, buf.at[k, 0, 0, :, left])
            gone(sem + 1, k, buf.at[k, pl.ds(0, 3), 0, :, left])
            gone(sem + 2, k, buf.at[k, pl.ds(0, 3), 0])
            gone(sem + 3, k, buf.at[k, :, 0, :, left])
        gone(11, k, crecv.at[k])
        gone(12, k, xsend.at[k])
        gone(13, k, zsend3.at[k])
        gone(14, k, zsend3.at[k])
        gone(15, k, low.at[k, 0, pl.ds(0, 3)])
        gone(16, k, low.at[k, 0])
        return 0

    lax.fori_loop(0, CHUNKS, drain, 0)
    pltpu.make_async_copy(gath, g_out, osem.at[0]).wait()
    pltpu.make_async_copy(plow, p_out, osem.at[1]).wait()
    pltpu.make_async_copy(products, d_out, osem.at[2]).wait()


def layer_sum():
    V = pltpu.VMEM
    return {
        "full": V((2, 4, 2, 16, LATS), F32),
        "send": V((CHUNKS, 4, 2, 16, LATS), BF16),
        "ya": V((CHUNKS, 3, 2, 16, HALF), BF16),
        "zb": V((CHUNKS, 4, 16, HALF), BF16),
        "za_send": V((CHUNKS, 16, HALF), BF16),
        "za": V((CHUNKS, 16, HALF), BF16),
        "mid": V((CHUNKS, 4, 16, HALF), BF16),
        "mid_f32": V((2, 4, 16, HALF), F32),
        "yb": V((CHUNKS, 3, 16, HALF), BF16),
        "keep": V((2, 16, HALF), F32),
    }


def exchange(acts, enc, enc_bias, dec, dec_bias):
    any_spec = pl.BlockSpec(memory_space=pl.ANY)
    vmem = pl.BlockSpec(memory_space=pltpu.VMEM)
    V = pltpu.VMEM
    by_latent = (CHUNKS, 2, 4, 16, WIDTH)
    by_layer = (CHUNKS, 4, 2, 16, LATS)
    return pl.pallas_call(
        step_kernel,
        out_shape=[
            jax.ShapeDtypeStruct(by_latent, BF16),
            jax.ShapeDtypeStruct(by_layer, BF16),
            jax.ShapeDtypeStruct((LATS, WIDTH), BF16),
            jax.ShapeDtypeStruct((8, WIDTH), F32),
            jax.ShapeDtypeStruct((8, LATS), F32),
        ],
        in_specs=[vmem, any_spec, vmem, any_spec, vmem],
        out_specs=[any_spec, any_spec, any_spec, vmem, vmem],
        scratch_shapes=[
            V((WIDTH, LATS), BF16), V((LATS, WIDTH), BF16), V((WIDTH, LATS), BF16),
            V(by_latent, BF16), V(by_layer, BF16), V(by_latent, BF16), V(by_layer, BF16),
            layer_sum(), layer_sum(), V((CHUNKS, 16, LATS), F32),
            V((2, 2, 4, 16, WIDTH), F32), V(by_latent, BF16), V((CHUNKS, 4, 16, WIDTH), BF16),
            V((CHUNKS, 3, 16, WIDTH), BF16), V((CHUNKS, 3, 16, WIDTH), BF16),
            V((CHUNKS, 16, PART), BF16), V((CHUNKS, 16, PART), BF16), V((2, 16, PART), F32),
            V((8, LATS), F32), V((LATS, 128), F32), V((LATS, 128), F32), V((8, LATS), F32),
            V((LATS, WIDTH), BF16),
            pltpu.SemaphoreType.DMA((SEMS, CHUNKS)),
            pltpu.SemaphoreType.DMA((SEMS, CHUNKS)),
            pltpu.SemaphoreType.DMA((2,)),
            pltpu.SemaphoreType.DMA((3,)),
        ],
        compiler_params=pltpu.CompilerParams(
            collective_id=0, has_side_effects=True, vmem_limit_bytes=60 << 20
        ),
        name="exchange",
    )(acts, enc, enc_bias, dec, dec_bias)


def rows_dot(left, right):
    return lax.dot_general(left, right, (((0,), (0,)), ((), ())), preferred_element_type=F32)


TILES = 4


def finish_kernel(
    g_hbm, p_hbm, d_hbm, low_sum, plow_sum,
    enc_out, enc_bias_out, dec_out, dec_bias_out,
    g, p, d, enc_stage, dec_stage, lsem, gsem, dsem, esem, wsem,
):
    wide, tall = WIDTH // TILES, LATS // TILES
    load_p = pltpu.make_async_copy(p_hbm, p, lsem.at[0])
    load_g, load_d = [], []
    for i in range(TILES):
        cols, rows = pl.ds(i * wide, wide), pl.ds(i * tall, tall)
        load_g.append(pltpu.make_async_copy(g_hbm.at[:, cols], g.at[:, cols], gsem.at[i]))
        load_d.append(pltpu.make_async_copy(d_hbm.at[rows], d.at[rows], dsem.at[i]))
    load_d[0].start()
    load_p.start()
    load_g[0].start()
    enc_bias_out[...] = jnp.sum(plow_sum[...], axis=0, keepdims=True)
    dec_bias_out[...] = jnp.sum(low_sum[...], axis=0, keepdims=True)
    writes = []

    def write(src, dst, sem):
        writes.append(pltpu.make_async_copy(src, dst, sem))
        writes[-1].start()

    for i in range(TILES):
        load_d[i].wait()
        if i + 1 < TILES:
            load_d[i + 1].start()
            load_g[i + 1].start()
        rows = pl.ds(i * tall, tall)
        for at in range(WIDTH // 128):
            dec_stage[i, pl.ds(at, tall, stride=WIDTH // 128), :] = d[rows, pl.ds(at * 128, 128)].astype(F32)
        lines = tall * (WIDTH // 128)
        write(dec_stage.at[i], dec_out.at[pl.ds(i * lines, lines)], wsem.at[i])
        if i == 0:
            load_p.wait()
        load_g[i].wait()
        rows = pl.ds(i * wide, wide)
        enc_stage[i] = rows_dot(g[:, rows], p[...])
        write(enc_stage.at[i], enc_out.at[rows], esem.at[i])
    for copy in writes:
        copy.wait()


def finish(g, p, d, low_sum, plow_sum):
    any_spec = pl.BlockSpec(memory_space=pl.ANY)
    vmem = pl.BlockSpec(memory_space=pltpu.VMEM)
    V = pltpu.VMEM
    lines = LATS * (WIDTH // 128)
    return pl.pallas_call(
        finish_kernel,
        out_shape=[
            jax.ShapeDtypeStruct((WIDTH, LATS), F32),
            jax.ShapeDtypeStruct((1, LATS), F32),
            jax.ShapeDtypeStruct((lines, 128), F32),
            jax.ShapeDtypeStruct((1, WIDTH), F32),
        ],
        in_specs=[any_spec] * 3 + [vmem] * 2,
        out_specs=[any_spec, vmem, any_spec, vmem],
        scratch_shapes=[
            V((TOKENS, WIDTH), BF16), V((TOKENS, LATS), BF16), V((LATS, WIDTH), BF16),
            V((TILES, WIDTH // TILES, LATS), F32), V((TILES, lines // TILES, 128), F32),
            pltpu.SemaphoreType.DMA((1,)),
            pltpu.SemaphoreType.DMA((TILES,)),
            pltpu.SemaphoreType.DMA((TILES,)),
            pltpu.SemaphoreType.DMA((TILES,)),
            pltpu.SemaphoreType.DMA((TILES,)),
        ],
        compiler_params=pltpu.CompilerParams(vmem_limit_bytes=56 << 20),
        name="finish",
    )(g, p, d, low_sum, plow_sum)


def on_device(acts, enc_weight, enc_bias, dec_weight, dec_bias):
    dec = dec_weight.reshape(LATS, WIDTH)
    g, p, d, low_sum, plow_sum = exchange(
        acts.reshape(TOKENS // 16, WIDTH), enc_weight.reshape(WIDTH, LATS), enc_bias.reshape(1, LATS), dec, dec_bias
    )
    g, p = g.reshape(TOKENS, WIDTH), p.reshape(TOKENS, LATS)
    enc_grad, enc_bias_grad, dec_grad, dec_bias_grad = finish(g, p, d, low_sum, plow_sum)
    return (
        enc_grad.reshape(1, WIDTH, LATS),
        enc_bias_grad.reshape(LATS),
        dec_grad.reshape(LATS, 1, WIDTH),
        dec_bias_grad,
    )


def solution(mesh):
    return jax.shard_map(
        on_device,
        mesh=mesh,
        in_specs=(
            P("latent", "layer", None),
            P("layer", None, "latent"),
            P("latent"),
            P("latent", "layer", None),
            P("layer", None),
        ),
        out_specs=(
            P("layer", None, "latent"),
            P("latent"),
            P("latent", "layer", None),
            P("layer", None),
        ),
        check_vma=False,
    )
```

```python
import functools
import math

import jax
import jax.numpy as jnp
from jax import lax
from jax.experimental import pallas as pl
from jax.experimental.pallas import tpu as pltpu
from jax.sharding import PartitionSpec as P

PENALTY = 0.05
EPS = 1e-06
MESH = pl.DeviceIdType.MESH
BF16 = jnp.bfloat16
F32 = jnp.float32

TOKENS = 1024
WIDTH = 2048
LATS = 1024
HALF = LATS // 2
PART = WIDTH // 2
CHUNKS = 8
ROWS = TOKENS // CHUNKS
SCALE = 1.0 / math.sqrt(TOKENS)
TILE = 512

SEMS = 25
FAR_FIRST = (2, 1, 3)

HOPS = (1.0,) * 17
STARTS = tuple(sum(HOPS[:m]) for m in range(len(HOPS) + 1))
LAGS = tuple(int(start) for start in STARTS)
ORDER = tuple(sorted(range(len(STARTS)), key=lambda m: (STARTS[m] % 1.0, -m)))


def before(first, second, ahead):
    at = (LAGS[first], ORDER.index(first))
    return at < (LAGS[second] + ahead, ORDER.index(second))


FULL = CHUNKS - 1 + LAGS[13]
assert FULL + 4 <= CHUNKS + LAGS[-1]
assert all(before(m, m + 1, 0) for m in range(len(HOPS)))
assert all(before(last, first, 2) for first, last in ((3, 4), (4, 5), (7, 9), (9, 10), (13, 14), (14, 15)))


def aligned(value, multiple):
    return pl.multiple_of(value, multiple)

CODE = 2.0**18
FLOOR = 2.0**-120


def pack(value):
    value = value * CODE
    return (value * value * (value * jnp.abs(value))).astype(BF16)


def unpack(coded):
    coded = coded.astype(F32)
    size = lax.rsqrt(lax.rsqrt(jnp.maximum(jnp.abs(coded), FLOOR))) * (1.0 / CODE)
    return jnp.where(coded < 0.0, -size, size)


def plain(value):
    return value.astype(BF16)


def widen(value):
    return value.astype(F32)


def step_kernel(
    acts, enc_hbm, enc_bias, dec_hbm, dec_bias,
    g_out, p_out, d_out, low_sum, plow_sum,
    enc, dec, dec_t, gath, codes, low, plow,
    sums1, sums2, active,
    full3, send3, crecv, xsend, xrecv, zsend3, zrecv3, keep3, norm_row, norm_wide, factor, code_sum, products,
    ssem, rsem, lsem, osem,
):
    a = lax.axis_index("layer")
    b = lax.axis_index("latent")
    zl, y = a // 4, a % 4
    x, zh, c = b // 4, (b // 2) % 2, b % 2

    def ydev(d):
        return (zl * 4 + (y + d) % 4, b)

    zldev = ((1 - zl) * 4 + y, b)

    def xdev(d):
        return (a, ((x + d) % 4) * 4 + zh * 2 + c)

    zhdev = (a, x * 4 + (1 - zh) * 2 + c)
    cdev = (a, x * 4 + zh * 2 + 1 - c)

    load_enc = pltpu.make_async_copy(enc_hbm, enc, lsem.at[0])
    load_dec = pltpu.make_async_copy(dec_hbm, dec, lsem.at[1])
    load_enc.start()
    load_dec.start()

    barrier = pltpu.get_barrier_semaphore()
    peers = [zldev, zhdev, cdev] + [ydev(d) for d in (1, 2, 3)] + [xdev(d) for d in (1, 2, 3)]
    for peer in peers:
        pl.semaphore_signal(barrier, inc=1, device_id=peer, device_id_type=MESH)
    pl.semaphore_wait(barrier, len(peers))

    def push(sem, k, src, dst, device):
        pltpu.make_async_remote_copy(
            src_ref=src, dst_ref=dst, send_sem=ssem.at[sem, k], recv_sem=rsem.at[sem, k],
            device_id=device, device_id_type=MESH,
        ).start()

    def arrived(sem, k, ref):
        pltpu.make_async_copy(ref, ref, rsem.at[sem, k]).wait()

    def gone(sem, k, ref):
        pltpu.make_async_copy(ref, ref, ssem.at[sem, k]).wait()

    left, right = pl.ds(0, HALF), pl.ds(HALF, HALF)
    lower, upper = pl.ds(0, PART), pl.ds(PART, PART)
    mine = pl.ds(aligned(zh * PART, PART), PART)
    theirs = pl.ds(aligned((1 - zh) * PART, PART), PART)

    def sum_send(sem, k, bufs, part):
        send, ya, zb = bufs["send"], bufs["ya"], bufs["zb"]
        if part == 0:
            for d in FAR_FIRST:
                push(sem, k, send.at[k, (y + d) % 4, :, :, left], ya.at[k, d - 1], ydev(d))
        else:
            push(sem + 1, k, send.at[k, :, 1 - zl, :, right], zb.at[k], zldev)

    def sum_mid(sem, k, bufs, narrow, wide):
        full, ya, zb, za_send, za, mid, mid_f32, yb, keep = (
            bufs[n] for n in ("full", "ya", "zb", "za_send", "za", "mid", "mid_f32", "yb", "keep")
        )
        arrived(sem + 1, k, zb.at[k])
        value = full[k % 2, :, zl, :, right] + wide(zb[k])
        mid_f32[k % 2] = value
        mid[k] = narrow(value)
        for d in FAR_FIRST:
            push(sem + 3, k, mid.at[k, (y + d) % 4], yb.at[k, d - 1], ydev(d))
        arrived(sem, k, ya.at[k])

        def total(half):
            value = full[k % 2, y, half, :, left]
            for d in range(3):
                value = value + wide(ya[k, d, half])
            return value

        za_send[k] = narrow(total(1 - zl))
        push(sem + 2, k, za_send.at[k], za.at[k], zldev)
        keep[k % 2] = total(zl)

    def sum_end(sem, k, bufs, wide):
        za, mid_f32, yb, keep = (bufs[n] for n in ("za", "mid_f32", "yb", "keep"))
        arrived(sem + 3, k, yb.at[k])
        second = mid_f32[k % 2, y]
        for d in range(3):
            second = second + wide(yb[k, d])
        arrived(sem + 2, k, za.at[k])
        return keep[k % 2] + wide(za[k]), second

    def spread_send(sem, k, buf):
        own, first = buf.at[k, y, zl], buf.at[k, y, zl, :, left]
        push(sem, k, first, first, zldev)
        for d in FAR_FIRST:
            push(sem + 2, k, own, own, ydev(d))

    def spread_mid(sem, k, buf):
        first = buf.at[k, y, 1 - zl, :, left]
        arrived(sem, k, first)
        for d in FAR_FIRST:
            push(sem + 1, k, first, first, ydev(d))
        arrived(sem + 2, k, buf.at[k, pl.ds(0, 3), 0])
        column = buf.at[k, :, zl, :, right]
        push(sem + 3, k, column, column, zldev)

    def spread_end(sem, k, buf):
        arrived(sem + 1, k, buf.at[k, pl.ds(0, 3), 0, :, left])
        arrived(sem + 3, k, buf.at[k, :, 0, :, right])

    def m0(pair):
        k = 2 * pair
        gath[k + zh, c, x] = acts[pl.ds(aligned(k * 8, 16), 16), :]
        ref = gath.at[k + zh, c, x]
        push(0, k, ref, ref, zhdev)
        for d in FAR_FIRST:
            push(1, k, ref, ref, xdev(d))

    def m1(pair):
        k = 2 * pair
        ref = gath.at[k + 1 - zh, c, x]
        arrived(0, k, ref)
        for d in FAR_FIRST:
            push(1, k, ref, ref, xdev(d))

    def m2(pair):
        k = 2 * pair
        arrived(1, k, gath.at[pl.ds(k, 2), 0, pl.ds(0, 3)])
        ref = gath.at[pl.ds(k, 2), c]
        push(2, k, ref, ref, cdev)

    def wait_pair(k):
        arrived(2, k, gath.at[pl.ds(k, 2), 1 - c])

    def m3(k):
        pl.when(k % 2 == 0)(functools.partial(wait_pair, k))
        pltpu.make_async_copy(gath.at[k], g_out.at[k], osem.at[0]).start()

        for part, cols in enumerate((left, right)):
            rows = gath[k].reshape(ROWS, WIDTH)
            value = jnp.dot(rows, enc[:, cols], preferred_element_type=F32).reshape(4, 2, 16, HALF)
            sums1["full"][k % 2, :, :, :, cols] = value
            sums1["send"][k, :, :, :, cols] = pack(value)
            sum_send(3, k, sums1, part)

    def m4(k):
        sum_mid(3, k, sums1, pack, unpack)

    def m5(k):
        for value, cols in zip(sum_end(3, k, sums1, unpack), (left, right)):
            value = jnp.maximum(value + enc_bias[:, cols], 0.0)
            active[k, :, cols] = value
            codes[k, y, zl, :, cols] = (value * value).astype(BF16)
        spread_send(7, k, codes)

    def m6(k):
        spread_mid(7, k, codes)

    def add_rows(total, k, rows):
        part = jnp.sum(rows.astype(F32).reshape(ROWS // 8, 8, rows.shape[1]), axis=0)
        total[...] = jnp.where(k == 0, part, total[...] + part)

    def m7(k):
        spread_end(7, k, codes)

        def tile(n, _):
            cols = pl.ds(aligned(n * TILE, TILE), TILE)
            rows = codes[k].reshape(ROWS, LATS)
            value = jnp.dot(rows, dec[:, cols], preferred_element_type=F32).reshape(2, 4, 16, TILE)
            full3[k % 2, :, :, :, cols] = value
            send3[k, :, :, :, cols] = value.astype(BF16)
            return 0

        lax.fori_loop(0, WIDTH // TILE, tile, 0)
        push(11, k, send3.at[k, 1 - c], crecv.at[k], cdev)
        add_rows(code_sum, k, codes[k].reshape(ROWS, LATS))

        @pl.when(k == CHUNKS - 1)
        def _():
            total = jnp.sum(code_sum[...], axis=0, keepdims=True) * (PENALTY * SCALE)
            factor[...] = jnp.broadcast_to(total, (128, LATS)).T / norm_wide[...]

    def m8(k):
        arrived(11, k, crecv.at[k])
        for d in FAR_FIRST:
            to = (x + d) % 4
            xsend[k, d - 1] = (full3[k % 2, c, to] + crecv[k, to].astype(F32)).astype(BF16)
            push(12, k, xsend.at[k, d - 1], xrecv.at[k, d - 1], xdev(d))

    def m9(k):
        arrived(12, k, xrecv.at[k])

        def total(cols):
            value = full3[k % 2, c, x, :, cols] + crecv[k, x, :, cols].astype(F32)
            for d in range(3):
                value = value + xrecv[k, d, :, cols].astype(F32)
            return value

        zsend3[k] = total(theirs).astype(BF16)
        push(13, k, zsend3.at[k], zrecv3.at[k], zhdev)
        keep3[k % 2] = total(mine)

    def m10(k):
        arrived(13, k, zrecv3.at[k])
        recon = keep3[k % 2] + zrecv3[k].astype(F32) + dec_bias[:, mine]
        flat = gath[k, c, x, :, mine].astype(F32)
        low[k, c, x, :, mine] = ((recon - flat) * SCALE).astype(BF16)
        ref = low.at[k, c, x, :, mine]
        push(14, k, ref, ref, zhdev)
        for d in FAR_FIRST:
            push(15, k, ref, ref, xdev(d))

    def m11(k):
        ref = low.at[k, c, x, :, theirs]
        arrived(14, k, ref)
        for d in FAR_FIRST:
            push(15, k, ref, ref, xdev(d))

    def m12(k):
        arrived(15, k, low.at[k, 0, pl.ds(0, 3)])
        ref = low.at[k, c]
        push(16, k, ref, ref, cdev)

    def m13(k):
        arrived(16, k, low.at[k, 1 - c])

        for part, cols in enumerate((left, right)):
            rows = low[k].reshape(ROWS, WIDTH)
            value = jnp.dot(rows, dec_t[:, cols], preferred_element_type=F32)
            value = (value + (PENALTY * SCALE) * norm_row[0:1, cols]).reshape(4, 2, 16, HALF)
            sums2["full"][k % 2, :, :, :, cols] = value
            sums2["send"][k, :, :, :, cols] = value.astype(BF16)
            sum_send(17, k, sums2, part)
        add_rows(low_sum, k, low[k].reshape(ROWS, WIDTH))

    def m14(k):
        sum_mid(17, k, sums2, plain, widen)

    def m15(k):
        for value, cols in zip(sum_end(17, k, sums2, widen), (left, right)):
            plow[k, y, zl, :, cols] = (value * (2.0 * active[k, :, cols])).astype(BF16)
        spread_send(21, k, plow)

    def m16(k):
        spread_mid(21, k, plow)

    def m17(k):
        spread_end(21, k, plow)
        pltpu.make_async_copy(plow.at[k], p_out.at[k], osem.at[1]).start()
        add_rows(plow_sum, k, plow[k].reshape(ROWS, LATS))

    def prepare(n):
        rows = pl.ds(aligned(n * 128, 128), 128)
        block = dec[rows, :]
        value = block.astype(F32)
        norm = jnp.sqrt(jnp.sum(value * value, axis=1, keepdims=True) + EPS)
        wide = jnp.broadcast_to(norm, (128, 128))
        norm_wide[rows, :] = wide
        norm_row[:, rows] = wide.T[0:8, :]
        dec_t[:, rows] = block.T

    def decoder_product(n):
        rows = pl.ds(aligned(n * (LATS // 4), LATS // 4), LATS // 4)
        left_side = codes[:, :, :, :, rows].reshape(TOKENS, LATS // 4)
        for half in (lower, upper):
            right_side = low[:, :, :, :, half].reshape(TOKENS, PART)
            value = rows_dot(left_side, right_side)
            penalty = jnp.tile(factor[rows, :], (1, PART // 128)) * dec[rows, half].astype(F32)
            products[rows, half] = (value + penalty).astype(BF16)
        pltpu.make_async_copy(products.at[rows], d_out.at[rows], osem.at[2]).start()

    stages = [m0, m1, m2, m3, m4, m5, m6, m7, m8, m9, m10, m11, m12, m13, m14, m15, m16, m17]

    def iteration(t, _):
        for m in ORDER:
            k = t - LAGS[m]
            if m == 3:
                pl.when(k == 0)(load_enc.wait)
            ready = jnp.logical_and(k >= 0, k < CHUNKS)
            if m < 3:
                ready = jnp.logical_and(ready, k % 2 == 0)
            pl.when(ready)(functools.partial(stages[m], k // 2 if m < 3 else k))
        @pl.when(jnp.logical_and(t >= FULL, t < FULL + 4))
        def _():
            decoder_product(t - FULL)

        pl.when(t == 0)(load_dec.wait)

        @pl.when(t < 4)
        def _():
            prepare(2 * t)
            prepare(2 * t + 1)

        return 0

    lax.fori_loop(0, CHUNKS + LAGS[-1], iteration, 0)

    def drain(k, _):
        @pl.when(k % 2 == 0)
        def _():
            gone(0, k, gath.at[k, 0, 0])
            gone(1, k, gath.at[pl.ds(k, 2), 0, pl.ds(0, 3)])
            gone(2, k, gath.at[pl.ds(k, 2), 0])

        for sem, bufs in ((3, sums1), (17, sums2)):
            gone(sem, k, bufs["ya"].at[k])
            gone(sem + 1, k, bufs["zb"].at[k])
            gone(sem + 2, k, bufs["za"].at[k])
            gone(sem + 3, k, bufs["yb"].at[k])
        for sem, buf in ((7, codes), (21, plow)):
            gone(sem, k, buf.at[k, 0, 0, :, left])
            gone(sem + 1, k, buf.at[k, pl.ds(0, 3), 0, :, left])
            gone(sem + 2, k, buf.at[k, pl.ds(0, 3), 0])
            gone(sem + 3, k, buf.at[k, :, 0, :, left])
        gone(11, k, crecv.at[k])
        gone(12, k, xsend.at[k])
        gone(13, k, zsend3.at[k])
        gone(14, k, zsend3.at[k])
        gone(15, k, low.at[k, 0, pl.ds(0, 3)])
        gone(16, k, low.at[k, 0])
        return 0

    lax.fori_loop(0, CHUNKS, drain, 0)
    pltpu.make_async_copy(gath, g_out, osem.at[0]).wait()
    pltpu.make_async_copy(plow, p_out, osem.at[1]).wait()
    pltpu.make_async_copy(products, d_out, osem.at[2]).wait()


def layer_sum():
    V = pltpu.VMEM
    return {
        "full": V((2, 4, 2, 16, LATS), F32),
        "send": V((CHUNKS, 4, 2, 16, LATS), BF16),
        "ya": V((CHUNKS, 3, 2, 16, HALF), BF16),
        "zb": V((CHUNKS, 4, 16, HALF), BF16),
        "za_send": V((CHUNKS, 16, HALF), BF16),
        "za": V((CHUNKS, 16, HALF), BF16),
        "mid": V((CHUNKS, 4, 16, HALF), BF16),
        "mid_f32": V((2, 4, 16, HALF), F32),
        "yb": V((CHUNKS, 3, 16, HALF), BF16),
        "keep": V((2, 16, HALF), F32),
    }


def exchange(acts, enc, enc_bias, dec, dec_bias):
    any_spec = pl.BlockSpec(memory_space=pl.ANY)
    vmem = pl.BlockSpec(memory_space=pltpu.VMEM)
    V = pltpu.VMEM
    by_latent = (CHUNKS, 2, 4, 16, WIDTH)
    by_layer = (CHUNKS, 4, 2, 16, LATS)
    return pl.pallas_call(
        step_kernel,
        out_shape=[
            jax.ShapeDtypeStruct(by_latent, BF16),
            jax.ShapeDtypeStruct(by_layer, BF16),
            jax.ShapeDtypeStruct((LATS, WIDTH), BF16),
            jax.ShapeDtypeStruct((8, WIDTH), F32),
            jax.ShapeDtypeStruct((8, LATS), F32),
        ],
        in_specs=[vmem, any_spec, vmem, any_spec, vmem],
        out_specs=[any_spec, any_spec, any_spec, vmem, vmem],
        scratch_shapes=[
            V((WIDTH, LATS), BF16), V((LATS, WIDTH), BF16), V((WIDTH, LATS), BF16),
            V(by_latent, BF16), V(by_layer, BF16), V(by_latent, BF16), V(by_layer, BF16),
            layer_sum(), layer_sum(), V((CHUNKS, 16, LATS), F32),
            V((2, 2, 4, 16, WIDTH), F32), V(by_latent, BF16), V((CHUNKS, 4, 16, WIDTH), BF16),
            V((CHUNKS, 3, 16, WIDTH), BF16), V((CHUNKS, 3, 16, WIDTH), BF16),
            V((CHUNKS, 16, PART), BF16), V((CHUNKS, 16, PART), BF16), V((2, 16, PART), F32),
            V((8, LATS), F32), V((LATS, 128), F32), V((LATS, 128), F32), V((8, LATS), F32),
            V((LATS, WIDTH), BF16),
            pltpu.SemaphoreType.DMA((SEMS, CHUNKS)),
            pltpu.SemaphoreType.DMA((SEMS, CHUNKS)),
            pltpu.SemaphoreType.DMA((2,)),
            pltpu.SemaphoreType.DMA((3,)),
        ],
        compiler_params=pltpu.CompilerParams(
            collective_id=0, has_side_effects=True, vmem_limit_bytes=60 << 20
        ),
        name="exchange",
    )(acts, enc, enc_bias, dec, dec_bias)


def rows_dot(left, right):
    return lax.dot_general(left, right, (((0,), (0,)), ((), ())), preferred_element_type=F32)


TILES = 4


def finish_kernel(
    g_hbm, p_hbm, d_hbm, low_sum, plow_sum,
    enc_out, enc_bias_out, dec_out, dec_bias_out,
    g, p, d, enc_stage, dec_stage, lsem, gsem, dsem, esem, wsem,
):
    wide, tall = WIDTH // TILES, LATS // TILES
    load_p = pltpu.make_async_copy(p_hbm, p, lsem.at[0])
    load_g, load_d = [], []
    for i in range(TILES):
        cols, rows = pl.ds(i * wide, wide), pl.ds(i * tall, tall)
        load_g.append(pltpu.make_async_copy(g_hbm.at[:, cols], g.at[:, cols], gsem.at[i]))
        load_d.append(pltpu.make_async_copy(d_hbm.at[rows], d.at[rows], dsem.at[i]))
    load_d[0].start()
    load_p.start()
    load_g[0].start()
    enc_bias_out[...] = jnp.sum(plow_sum[...], axis=0, keepdims=True)
    dec_bias_out[...] = jnp.sum(low_sum[...], axis=0, keepdims=True)
    writes = []

    def write(src, dst, sem):
        writes.append(pltpu.make_async_copy(src, dst, sem))
        writes[-1].start()

    for i in range(TILES):
        load_d[i].wait()
        if i + 1 < TILES:
            load_d[i + 1].start()
            load_g[i + 1].start()
        rows = pl.ds(i * tall, tall)
        for at in range(WIDTH // 128):
            dec_stage[i, pl.ds(at, tall, stride=WIDTH // 128), :] = d[rows, pl.ds(at * 128, 128)].astype(F32)
        lines = tall * (WIDTH // 128)
        write(dec_stage.at[i], dec_out.at[pl.ds(i * lines, lines)], wsem.at[i])
        if i == 0:
            load_p.wait()
        load_g[i].wait()
        rows = pl.ds(i * wide, wide)
        enc_stage[i] = rows_dot(g[:, rows], p[...])
        write(enc_stage.at[i], enc_out.at[rows], esem.at[i])
    for copy in writes:
        copy.wait()


def finish(g, p, d, low_sum, plow_sum):
    any_spec = pl.BlockSpec(memory_space=pl.ANY)
    vmem = pl.BlockSpec(memory_space=pltpu.VMEM)
    V = pltpu.VMEM
    lines = LATS * (WIDTH // 128)
    return pl.pallas_call(
        finish_kernel,
        out_shape=[
            jax.ShapeDtypeStruct((WIDTH, LATS), F32),
            jax.ShapeDtypeStruct((1, LATS), F32),
            jax.ShapeDtypeStruct((lines, 128), F32),
            jax.ShapeDtypeStruct((1, WIDTH), F32),
        ],
        in_specs=[any_spec] * 3 + [vmem] * 2,
        out_specs=[any_spec, vmem, any_spec, vmem],
        scratch_shapes=[
            V((TOKENS, WIDTH), BF16), V((TOKENS, LATS), BF16), V((LATS, WIDTH), BF16),
            V((TILES, WIDTH // TILES, LATS), F32), V((TILES, lines // TILES, 128), F32),
            pltpu.SemaphoreType.DMA((1,)),
            pltpu.SemaphoreType.DMA((TILES,)),
            pltpu.SemaphoreType.DMA((TILES,)),
            pltpu.SemaphoreType.DMA((TILES,)),
            pltpu.SemaphoreType.DMA((TILES,)),
        ],
        compiler_params=pltpu.CompilerParams(vmem_limit_bytes=56 << 20),
        name="finish",
    )(g, p, d, low_sum, plow_sum)


def on_device(acts, enc_weight, enc_bias, dec_weight, dec_bias):
    dec = dec_weight.reshape(LATS, WIDTH)
    g, p, d, low_sum, plow_sum = exchange(
        acts.reshape(TOKENS // 16, WIDTH), enc_weight.reshape(WIDTH, LATS), enc_bias.reshape(1, LATS), dec, dec_bias
    )
    g, p = g.reshape(TOKENS, WIDTH), p.reshape(TOKENS, LATS)
    enc_grad, enc_bias_grad, dec_grad, dec_bias_grad = finish(g, p, d, low_sum, plow_sum)
    return (
        enc_grad.reshape(1, WIDTH, LATS),
        enc_bias_grad.reshape(LATS),
        dec_grad.reshape(LATS, 1, WIDTH),
        dec_bias_grad,
    )


def solution(mesh):
    return jax.shard_map(
        on_device,
        mesh=mesh,
        in_specs=(
            P("latent", "layer", None),
            P("layer", None, "latent"),
            P("latent"),
            P("latent", "layer", None),
            P("layer", None),
        ),
        out_specs=(
            P("layer", None, "latent"),
            P("latent"),
            P("latent", "layer", None),
            P("layer", None),
        ),
        check_vma=False,
    )
```

```python
import functools
import math

import jax
import jax.numpy as jnp
from jax import lax
from jax.experimental import pallas as pl
from jax.experimental.pallas import tpu as pltpu
from jax.sharding import PartitionSpec as P

PENALTY = 0.05
EPS = 1e-06
MESH = pl.DeviceIdType.MESH
BF16 = jnp.bfloat16
F32 = jnp.float32

TOKENS = 1024
WIDTH = 2048
LATS = 1024
HALF = LATS // 2
PART = WIDTH // 2
FIRST = 768
REST = PART - FIRST
CHUNKS = 8
ROWS = TOKENS // CHUNKS
SCALE = 1.0 / math.sqrt(TOKENS)
TILE = 512

SEMS = 27
FAR_FIRST = (2, 1, 3)

HOPS = (1.0,) * 17
STARTS = tuple(sum(HOPS[:m]) for m in range(len(HOPS) + 1))
LAGS = tuple(int(start) for start in STARTS)
ORDER = tuple(sorted(range(len(STARTS)), key=lambda m: (STARTS[m] % 1.0, -m)))


def before(first, second, ahead):
    at = (LAGS[first], ORDER.index(first))
    return at < (LAGS[second] + ahead, ORDER.index(second))


FULL = CHUNKS - 1 + LAGS[13]
assert FULL + 4 <= CHUNKS + LAGS[-1]
assert all(before(m, m + 1, 0) for m in range(len(HOPS)))
assert all(before(last, first, 2) for first, last in ((3, 4), (4, 5), (7, 9), (9, 10), (13, 14), (14, 15)))


def aligned(value, multiple):
    return pl.multiple_of(value, multiple)

CODE = 2.0**18
FLOOR = 2.0**-120


def pack(value):
    value = value * CODE
    return (value * value * (value * jnp.abs(value))).astype(BF16)


def unpack(coded):
    coded = coded.astype(F32)
    size = lax.rsqrt(lax.rsqrt(jnp.maximum(jnp.abs(coded), FLOOR))) * (1.0 / CODE)
    return jnp.where(coded < 0.0, -size, size)


def plain(value):
    return value.astype(BF16)


def widen(value):
    return value.astype(F32)


def step_kernel(
    acts_hbm, enc_hbm, enc_bias, dec_hbm, dec_bias,
    g_out, p_out, d_out, low_sum, plow_sum,
    acts, enc, dec, dec_t, gath, codes, low, plow,
    sums1, sums2, active,
    full3, send3, crecv, xsend, xrecv, zsend3, zrecv3, zb_send, zb_recv, xb_send, xb_recv, keep3, keep_rest, norm_row, norm_wide, factor, code_sum, spread, products,
    ssem, rsem, lsem, osem,
):
    a = lax.axis_index("layer")
    b = lax.axis_index("latent")
    zl, y = a // 4, a % 4
    x, zh, c = b // 4, (b // 2) % 2, b % 2

    def ydev(d):
        return (zl * 4 + (y + d) % 4, b)

    zldev = ((1 - zl) * 4 + y, b)

    def xdev(d):
        return (a, ((x + d) % 4) * 4 + zh * 2 + c)

    zhdev = (a, x * 4 + (1 - zh) * 2 + c)
    cdev = (a, x * 4 + zh * 2 + 1 - c)

    barrier = pltpu.get_barrier_semaphore()
    peers = [zldev, zhdev, cdev] + [ydev(d) for d in (1, 2, 3)] + [xdev(d) for d in (1, 2, 3)]
    for peer in peers:
        pl.semaphore_signal(barrier, inc=1, device_id=peer, device_id_type=MESH)
    load_acts = pltpu.make_async_copy(acts_hbm, acts, lsem.at[2])
    load_enc = pltpu.make_async_copy(enc_hbm, enc, lsem.at[0])
    load_dec = pltpu.make_async_copy(dec_hbm, dec, lsem.at[1])
    load_acts.start()
    load_enc.start()
    load_dec.start()
    load_acts.wait()
    pl.semaphore_wait(barrier, len(peers))

    def push(sem, k, src, dst, device):
        pltpu.make_async_remote_copy(
            src_ref=src, dst_ref=dst, send_sem=ssem.at[sem, k], recv_sem=rsem.at[sem, k],
            device_id=device, device_id_type=MESH,
        ).start()

    def arrived(sem, k, ref):
        pltpu.make_async_copy(ref, ref, rsem.at[sem, k]).wait()

    def gone(sem, k, ref):
        pltpu.make_async_copy(ref, ref, ssem.at[sem, k]).wait()

    left, right = pl.ds(0, HALF), pl.ds(HALF, HALF)
    lower, upper = pl.ds(0, PART), pl.ds(PART, PART)
    mine = pl.ds(aligned(zh * PART, PART), PART)
    theirs = pl.ds(aligned((1 - zh) * PART, PART), PART)

    def sum_send(sem, k, bufs, part):
        send, ya, zb = bufs["send"], bufs["ya"], bufs["zb"]
        if part == 0:
            for d in FAR_FIRST:
                push(sem, k, send.at[k, (y + d) % 4, :, :, left], ya.at[k, d - 1], ydev(d))
        else:
            push(sem + 1, k, send.at[k, :, 1 - zl, :, right], zb.at[k], zldev)

    def sum_mid(sem, k, bufs, narrow, wide):
        full, ya, zb, za_send, za, mid, mid_f32, yb, keep = (
            bufs[n] for n in ("full", "ya", "zb", "za_send", "za", "mid", "mid_f32", "yb", "keep")
        )
        arrived(sem + 1, k, zb.at[k])
        value = full[k % 2, :, zl, :, right] + wide(zb[k])
        mid_f32[k % 2] = value
        mid[k] = narrow(value)
        for d in FAR_FIRST:
            push(sem + 3, k, mid.at[k, (y + d) % 4], yb.at[k, d - 1], ydev(d))
        arrived(sem, k, ya.at[k])

        def total(half):
            value = full[k % 2, y, half, :, left]
            for d in range(3):
                value = value + wide(ya[k, d, half])
            return value

        za_send[k] = narrow(total(1 - zl))
        push(sem + 2, k, za_send.at[k], za.at[k], zldev)
        keep[k % 2] = total(zl)

    def sum_end(sem, k, bufs, wide):
        za, mid_f32, yb, keep = (bufs[n] for n in ("za", "mid_f32", "yb", "keep"))
        arrived(sem + 3, k, yb.at[k])
        second = mid_f32[k % 2, y]
        for d in range(3):
            second = second + wide(yb[k, d])
        arrived(sem + 2, k, za.at[k])
        return keep[k % 2] + wide(za[k]), second

    def spread_send(sem, k, buf):
        own, first = buf.at[k, y, zl], buf.at[k, y, zl, :, left]
        push(sem, k, first, first, zldev)
        for d in FAR_FIRST:
            push(sem + 2, k, own, own, ydev(d))

    def spread_mid(sem, k, buf):
        first = buf.at[k, y, 1 - zl, :, left]
        arrived(sem, k, first)
        for d in FAR_FIRST:
            push(sem + 1, k, first, first, ydev(d))
        arrived(sem + 2, k, buf.at[k, pl.ds(0, 3), 0])
        column = buf.at[k, :, zl, :, right]
        push(sem + 3, k, column, column, zldev)

    def spread_end(sem, k, buf):
        arrived(sem + 1, k, buf.at[k, pl.ds(0, 3), 0, :, left])
        arrived(sem + 3, k, buf.at[k, :, 0, :, right])

    def m0(pair):
        k = 2 * pair
        gath[k + zh, c, x] = acts[pl.ds(aligned(k * 8, 16), 16), :]
        ref = gath.at[k + zh, c, x]
        push(0, k, ref, ref, zhdev)
        for d in FAR_FIRST:
            push(1, k, ref, ref, xdev(d))

    def m1(pair):
        k = 2 * pair
        ref = gath.at[k + 1 - zh, c, x]
        arrived(0, k, ref)
        for d in FAR_FIRST:
            push(1, k, ref, ref, xdev(d))

    def m2(pair):
        k = 2 * pair
        arrived(1, k, gath.at[pl.ds(k, 2), 0, pl.ds(0, 3)])
        ref = gath.at[pl.ds(k, 2), c]
        push(2, k, ref, ref, cdev)

    def wait_pair(k):
        arrived(2, k, gath.at[pl.ds(k, 2), 1 - c])

    def m3(k):
        pl.when(k % 2 == 0)(functools.partial(wait_pair, k))
        pltpu.make_async_copy(gath.at[k], g_out.at[k], osem.at[0]).start()

        for part, cols in enumerate((left, right)):
            rows = gath[k].reshape(ROWS, WIDTH)
            value = jnp.dot(rows, enc[:, cols], preferred_element_type=F32).reshape(4, 2, 16, HALF)
            sums1["full"][k % 2, :, :, :, cols] = value
            sums1["send"][k, :, :, :, cols] = pack(value)
            sum_send(3, k, sums1, part)

    def m4(k):
        sum_mid(3, k, sums1, pack, unpack)

    def m5(k):
        for value, cols in zip(sum_end(3, k, sums1, unpack), (left, right)):
            value = jnp.maximum(value + enc_bias[:, cols], 0.0)
            active[k, :, cols] = value
            codes[k, y, zl, :, cols] = (value * value).astype(BF16)
        spread_send(7, k, codes)

    def m6(k):
        spread_mid(7, k, codes)

    def add_rows(total, k, rows):
        part = jnp.sum(rows.astype(F32).reshape(ROWS // 8, 8, rows.shape[1]), axis=0)
        total[...] = jnp.where(k == 0, part, total[...] + part)

    def m7(k):
        spread_end(7, k, codes)

        def tile(n, _):
            cols = pl.ds(aligned(n * TILE, TILE), TILE)
            rows = codes[k].reshape(ROWS, LATS)
            value = jnp.dot(rows, dec[:, cols], preferred_element_type=F32).reshape(2, 4, 16, TILE)
            full3[k % 2, :, :, :, cols] = value
            send3[k, :, :, :, cols] = value.astype(BF16)
            return 0

        lax.fori_loop(0, WIDTH // TILE, tile, 0)
        push(11, k, send3.at[k, 1 - c], crecv.at[k], cdev)
        add_rows(code_sum, k, codes[k].reshape(ROWS, LATS))

        @pl.when(k == CHUNKS - 1)
        def _():
            total = jnp.sum(code_sum[...], axis=0, keepdims=True) * (PENALTY * SCALE)
            factor[...] = jnp.broadcast_to(total, (128, LATS)).T / norm_wide[...]

    def pair_sum(k, block, cols):
        return full3[k % 2, c, block, :, cols] + crecv[k, block, :, cols].astype(F32)

    def first_of(half):
        return pl.ds(aligned(half * PART, PART), FIRST)

    def rest_of(half):
        return pl.ds(aligned(half * PART + FIRST, REST), REST)

    def m8(k):
        arrived(11, k, crecv.at[k])
        for d in FAR_FIRST:
            to = (x + d) % 4
            for half in range(2):
                xsend[k, d - 1, :, pl.ds(half * FIRST, FIRST)] = pair_sum(k, to, first_of(half)).astype(BF16)
            push(12, k, xsend.at[k, d - 1], xrecv.at[k, d - 1], xdev(d))
        for block in range(4):
            zb_send[k, block] = pair_sum(k, block, rest_of(1 - zh)).astype(BF16)
        push(25, k, zb_send.at[k], zb_recv.at[k], zhdev)

    def m9(k):
        arrived(25, k, zb_recv.at[k])
        for d in FAR_FIRST:
            to = (x + d) % 4
            value = pair_sum(k, to, rest_of(zh)) + zb_recv[k, to].astype(F32)
            xb_send[k, d - 1] = value.astype(BF16)
            push(26, k, xb_send.at[k, d - 1], xb_recv.at[k, d - 1], xdev(d))
        keep_rest[k % 2] = pair_sum(k, x, rest_of(zh)) + zb_recv[k, x].astype(F32)
        arrived(12, k, xrecv.at[k])

        def total(half):
            value = pair_sum(k, x, first_of(half))
            for d in range(3):
                value = value + xrecv[k, d, :, pl.ds(aligned(half * FIRST, FIRST), FIRST)].astype(F32)
            return value

        zsend3[k] = total(1 - zh).astype(BF16)
        push(13, k, zsend3.at[k], zrecv3.at[k], zhdev)
        keep3[k % 2] = total(zh)

    def m10(k):
        arrived(26, k, xb_recv.at[k])
        rest = keep_rest[k % 2]
        for d in range(3):
            rest = rest + xb_recv[k, d].astype(F32)
        arrived(13, k, zrecv3.at[k])
        first = keep3[k % 2] + zrecv3[k].astype(F32)
        for recon, cols in ((first, first_of(zh)), (rest, rest_of(zh))):
            flat = gath[k, c, x, :, cols].astype(F32)
            low[k, c, x, :, cols] = ((recon + dec_bias[:, cols] - flat) * SCALE).astype(BF16)
        ref = low.at[k, c, x, :, mine]
        push(14, k, ref, ref, zhdev)
        for d in FAR_FIRST:
            push(15, k, ref, ref, xdev(d))

    def m11(k):
        ref = low.at[k, c, x, :, theirs]
        arrived(14, k, ref)
        for d in FAR_FIRST:
            push(15, k, ref, ref, xdev(d))

    def m12(k):
        arrived(15, k, low.at[k, 0, pl.ds(0, 3)])
        ref = low.at[k, c]
        push(16, k, ref, ref, cdev)

    def m13(k):
        arrived(16, k, low.at[k, 1 - c])

        for part, cols in enumerate((left, right)):
            rows = low[k].reshape(ROWS, WIDTH)
            value = jnp.dot(rows, dec_t[:, cols], preferred_element_type=F32)
            value = (value + (PENALTY * SCALE) * norm_row[0:1, cols]).reshape(4, 2, 16, HALF)
            sums2["full"][k % 2, :, :, :, cols] = value
            sums2["send"][k, :, :, :, cols] = value.astype(BF16)
            sum_send(17, k, sums2, part)
        add_rows(low_sum, k, low[k].reshape(ROWS, WIDTH))

    def m14(k):
        sum_mid(17, k, sums2, plain, widen)

    def m15(k):
        for value, cols in zip(sum_end(17, k, sums2, widen), (left, right)):
            plow[k, y, zl, :, cols] = (value * (2.0 * active[k, :, cols])).astype(BF16)
        spread_send(21, k, plow)

    def m16(k):
        spread_mid(21, k, plow)

    def m17(k):
        spread_end(21, k, plow)
        pltpu.make_async_copy(plow.at[k], p_out.at[k], osem.at[1]).start()
        add_rows(plow_sum, k, plow[k].reshape(ROWS, LATS))

    def prepare(n):
        rows = pl.ds(aligned(n * 128, 128), 128)
        block = dec[rows, :]
        value = block.astype(F32)
        norm = jnp.sqrt(jnp.sum(value * value, axis=1, keepdims=True) + EPS)
        wide = jnp.broadcast_to(norm, (128, 128))
        norm_wide[rows, :] = wide
        norm_row[:, rows] = wide.T[0:8, :]
        dec_t[:, rows] = block.T

    lines = LATS * (WIDTH // 128) // 4

    def product_out(n):
        part = pl.ds(aligned(n * lines, lines), lines)
        return part, pltpu.make_async_copy(products.at[part], d_out.at[part], osem.at[2])

    def decoder_product(n):
        rows = pl.ds(aligned(n * (LATS // 4), LATS // 4), LATS // 4)
        left_side = codes[:, :, :, :, rows].reshape(TOKENS, LATS // 4)
        for half in range(2):
            right_side = low[:, :, :, :, pl.ds(half * PART, PART)].reshape(TOKENS, PART)
            value = rows_dot(left_side, right_side)
            for j in range(PART // 128):
                at = half * (PART // 128) + j
                part = value[:, j * 128 : (j + 1) * 128]
                part = part + factor[rows, :] * dec[rows, pl.ds(at * 128, 128)].astype(F32)
                spread[pl.ds(at, LATS // 4, stride=WIDTH // 128), :] = part
        part, out = product_out(n)
        products[part, :] = spread[...].astype(BF16)
        out.start()

    stages = [m0, m1, m2, m3, m4, m5, m6, m7, m8, m9, m10, m11, m12, m13, m14, m15, m16, m17]

    def iteration(t, _):
        for m in ORDER:
            k = t - LAGS[m]
            if m == 3:
                pl.when(k == 0)(load_enc.wait)
            ready = jnp.logical_and(k >= 0, k < CHUNKS)
            if m < 3:
                ready = jnp.logical_and(ready, k % 2 == 0)
            pl.when(ready)(functools.partial(stages[m], k // 2 if m < 3 else k))
        @pl.when(jnp.logical_and(t >= FULL, t < FULL + 4))
        def _():
            decoder_product(t - FULL)

        pl.when(t == 0)(load_dec.wait)

        @pl.when(t < 4)
        def _():
            prepare(2 * t)
            prepare(2 * t + 1)

        return 0

    lax.fori_loop(0, CHUNKS + LAGS[-1], iteration, 0)

    def drain(k, _):
        @pl.when(k % 2 == 0)
        def _():
            gone(0, k, gath.at[k, 0, 0])
            gone(1, k, gath.at[pl.ds(k, 2), 0, pl.ds(0, 3)])
            gone(2, k, gath.at[pl.ds(k, 2), 0])

        for sem, bufs in ((3, sums1), (17, sums2)):
            gone(sem, k, bufs["ya"].at[k])
            gone(sem + 1, k, bufs["zb"].at[k])
            gone(sem + 2, k, bufs["za"].at[k])
            gone(sem + 3, k, bufs["yb"].at[k])
        for sem, buf in ((7, codes), (21, plow)):
            gone(sem, k, buf.at[k, 0, 0, :, left])
            gone(sem + 1, k, buf.at[k, pl.ds(0, 3), 0, :, left])
            gone(sem + 2, k, buf.at[k, pl.ds(0, 3), 0])
            gone(sem + 3, k, buf.at[k, :, 0, :, left])
        gone(11, k, crecv.at[k])
        gone(12, k, xsend.at[k])
        gone(13, k, zsend3.at[k])
        gone(14, k, low.at[k, 0, 0, :, lower])
        gone(25, k, zb_send.at[k])
        gone(26, k, xb_send.at[k])
        gone(15, k, low.at[k, 0, pl.ds(0, 3)])
        gone(16, k, low.at[k, 0])
        return 0

    lax.fori_loop(0, CHUNKS, drain, 0)
    pltpu.make_async_copy(gath, g_out, osem.at[0]).wait()
    pltpu.make_async_copy(plow, p_out, osem.at[1]).wait()
    pltpu.make_async_copy(products, d_out, osem.at[2]).wait()


def layer_sum():
    V = pltpu.VMEM
    return {
        "full": V((2, 4, 2, 16, LATS), F32),
        "send": V((CHUNKS, 4, 2, 16, LATS), BF16),
        "ya": V((CHUNKS, 3, 2, 16, HALF), BF16),
        "zb": V((CHUNKS, 4, 16, HALF), BF16),
        "za_send": V((CHUNKS, 16, HALF), BF16),
        "za": V((CHUNKS, 16, HALF), BF16),
        "mid": V((CHUNKS, 4, 16, HALF), BF16),
        "mid_f32": V((2, 4, 16, HALF), F32),
        "yb": V((CHUNKS, 3, 16, HALF), BF16),
        "keep": V((2, 16, HALF), F32),
    }


def exchange(acts, enc, enc_bias, dec, dec_bias):
    any_spec = pl.BlockSpec(memory_space=pl.ANY)
    vmem = pl.BlockSpec(memory_space=pltpu.VMEM)
    V = pltpu.VMEM
    by_latent = (CHUNKS, 2, 4, 16, WIDTH)
    by_layer = (CHUNKS, 4, 2, 16, LATS)
    return pl.pallas_call(
        step_kernel,
        out_shape=[
            jax.ShapeDtypeStruct(by_latent, BF16),
            jax.ShapeDtypeStruct(by_layer, BF16),
            jax.ShapeDtypeStruct((LATS * (WIDTH // 128), 128), BF16),
            jax.ShapeDtypeStruct((8, WIDTH), F32),
            jax.ShapeDtypeStruct((8, LATS), F32),
        ],
        in_specs=[any_spec, any_spec, vmem, any_spec, vmem],
        out_specs=[any_spec, any_spec, any_spec, vmem, vmem],
        scratch_shapes=[
            V((TOKENS // 16, WIDTH), BF16),
            V((WIDTH, LATS), BF16), V((LATS, WIDTH), BF16), V((WIDTH, LATS), BF16),
            V(by_latent, BF16), V(by_layer, BF16), V(by_latent, BF16), V(by_layer, BF16),
            layer_sum(), layer_sum(), V((CHUNKS, 16, LATS), F32),
            V((2, 2, 4, 16, WIDTH), F32), V(by_latent, BF16), V((CHUNKS, 4, 16, WIDTH), BF16),
            V((CHUNKS, 3, 16, 2 * FIRST), BF16), V((CHUNKS, 3, 16, 2 * FIRST), BF16),
            V((CHUNKS, 16, FIRST), BF16), V((CHUNKS, 16, FIRST), BF16),
            V((CHUNKS, 4, 16, REST), BF16), V((CHUNKS, 4, 16, REST), BF16),
            V((CHUNKS, 3, 16, REST), BF16), V((CHUNKS, 3, 16, REST), BF16),
            V((2, 16, FIRST), F32), V((2, 16, REST), F32),
            V((8, LATS), F32), V((LATS, 128), F32), V((LATS, 128), F32), V((8, LATS), F32),
            V((LATS * (WIDTH // 128) // 4, 128), F32), V((LATS * (WIDTH // 128), 128), BF16),
            pltpu.SemaphoreType.DMA((SEMS, CHUNKS)),
            pltpu.SemaphoreType.DMA((SEMS, CHUNKS)),
            pltpu.SemaphoreType.DMA((3,)),
            pltpu.SemaphoreType.DMA((3,)),
        ],
        compiler_params=pltpu.CompilerParams(
            collective_id=0, has_side_effects=True, vmem_limit_bytes=60 << 20
        ),
        name="exchange",
    )(acts, enc, enc_bias, dec, dec_bias)


def rows_dot(left, right):
    return lax.dot_general(left, right, (((0,), (0,)), ((), ())), preferred_element_type=F32)


TILES = 4


def finish_kernel(
    g_hbm, p_hbm, d_hbm, low_sum, plow_sum,
    enc_out, enc_bias_out, dec_out, dec_bias_out,
    g, p, d, enc_stage, dec_stage, lsem, gsem, dsem, esem, wsem,
):
    wide, tall = WIDTH // TILES, LATS * (WIDTH // 128) // TILES
    load_p = pltpu.make_async_copy(p_hbm, p, lsem.at[0])
    load_g, load_d = [], []
    for i in range(TILES):
        cols, rows = pl.ds(i * wide, wide), pl.ds(i * tall, tall)
        load_g.append(pltpu.make_async_copy(g_hbm.at[:, cols], g.at[:, cols], gsem.at[i]))
        load_d.append(pltpu.make_async_copy(d_hbm.at[rows], d.at[rows], dsem.at[i]))
    load_d[0].start()
    load_p.start()
    load_g[0].start()
    enc_bias_out[...] = jnp.sum(plow_sum[...], axis=0, keepdims=True)
    dec_bias_out[...] = jnp.sum(low_sum[...], axis=0, keepdims=True)
    writes = []

    def write(src, dst, sem):
        writes.append(pltpu.make_async_copy(src, dst, sem))
        writes[-1].start()

    for i in range(TILES):
        load_d[i].wait()
        if i + 1 < TILES:
            load_d[i + 1].start()
            load_g[i + 1].start()
        rows = pl.ds(i * tall, tall)
        dec_stage[i] = d[rows, :].astype(F32)
        write(dec_stage.at[i], dec_out.at[rows], wsem.at[i])
        if i == 0:
            load_p.wait()
        load_g[i].wait()
        rows = pl.ds(i * wide, wide)
        enc_stage[i] = rows_dot(g[:, rows], p[...])
        write(enc_stage.at[i], enc_out.at[rows], esem.at[i])
    for copy in writes:
        copy.wait()


def finish(g, p, d, low_sum, plow_sum):
    any_spec = pl.BlockSpec(memory_space=pl.ANY)
    vmem = pl.BlockSpec(memory_space=pltpu.VMEM)
    V = pltpu.VMEM
    lines = LATS * (WIDTH // 128)
    return pl.pallas_call(
        finish_kernel,
        out_shape=[
            jax.ShapeDtypeStruct((WIDTH, LATS), F32),
            jax.ShapeDtypeStruct((1, LATS), F32),
            jax.ShapeDtypeStruct((lines, 128), F32),
            jax.ShapeDtypeStruct((1, WIDTH), F32),
        ],
        in_specs=[any_spec] * 3 + [vmem] * 2,
        out_specs=[any_spec, vmem, any_spec, vmem],
        scratch_shapes=[
            V((TOKENS, WIDTH), BF16), V((TOKENS, LATS), BF16), V((lines, 128), BF16),
            V((TILES, WIDTH // TILES, LATS), F32), V((TILES, lines // TILES, 128), F32),
            pltpu.SemaphoreType.DMA((1,)),
            pltpu.SemaphoreType.DMA((TILES,)),
            pltpu.SemaphoreType.DMA((TILES,)),
            pltpu.SemaphoreType.DMA((TILES,)),
            pltpu.SemaphoreType.DMA((TILES,)),
        ],
        compiler_params=pltpu.CompilerParams(vmem_limit_bytes=56 << 20),
        name="finish",
    )(g, p, d, low_sum, plow_sum)


def on_device(acts, enc_weight, enc_bias, dec_weight, dec_bias):
    dec = dec_weight.reshape(LATS, WIDTH)
    g, p, d, low_sum, plow_sum = exchange(
        acts.reshape(TOKENS // 16, WIDTH), enc_weight.reshape(WIDTH, LATS), enc_bias.reshape(1, LATS), dec, dec_bias
    )
    g, p = g.reshape(TOKENS, WIDTH), p.reshape(TOKENS, LATS)
    enc_grad, enc_bias_grad, dec_grad, dec_bias_grad = finish(g, p, d, low_sum, plow_sum)
    return (
        enc_grad.reshape(1, WIDTH, LATS),
        enc_bias_grad.reshape(LATS),
        dec_grad.reshape(LATS, 1, WIDTH),
        dec_bias_grad,
    )


def solution(mesh):
    return jax.shard_map(
        on_device,
        mesh=mesh,
        in_specs=(
            P("latent", "layer", None),
            P("layer", None, "latent"),
            P("latent"),
            P("latent", "layer", None),
            P("layer", None),
        ),
        out_specs=(
            P("layer", None, "latent"),
            P("latent"),
            P("latent", "layer", None),
            P("layer", None),
        ),
        check_vma=False,
    )
```

```python
import functools
import math

import jax
import jax.numpy as jnp
from jax import lax
from jax.experimental import pallas as pl
from jax.experimental.pallas import tpu as pltpu
from jax.sharding import PartitionSpec as P

PENALTY = 0.05
EPS = 1e-06
MESH = pl.DeviceIdType.MESH
BF16 = jnp.bfloat16
F32 = jnp.float32

TOKENS = 1024
WIDTH = 2048
LATS = 1024
HALF = LATS // 2
PART = WIDTH // 2
FIRST = 768
REST = PART - FIRST
CHUNKS = 8
ROWS = TOKENS // CHUNKS
SCALE = 1.0 / math.sqrt(TOKENS)
TILE = 512

SEMS = 27
FAR_FIRST = (2, 1, 3)

HOPS = (1.0,) * 17
STARTS = tuple(sum(HOPS[:m]) for m in range(len(HOPS) + 1))
LAGS = tuple(int(start) for start in STARTS)
ORDER = tuple(sorted(range(len(STARTS)), key=lambda m: (STARTS[m] % 1.0, -m)))


def before(first, second, ahead):
    at = (LAGS[first], ORDER.index(first))
    return at < (LAGS[second] + ahead, ORDER.index(second))


FULL = CHUNKS - 1 + LAGS[13]
assert FULL + 4 <= CHUNKS + LAGS[-1]
assert all(before(m, m + 1, 0) for m in range(len(HOPS)))
assert all(before(last, first, 2) for first, last in ((3, 4), (4, 5), (7, 9), (9, 10), (13, 14), (14, 15)))


def aligned(value, multiple):
    return pl.multiple_of(value, multiple)

CODE = 2.0**18
FLOOR = 2.0**-120


def pack(value):
    value = value * CODE
    return (value * value * (value * jnp.abs(value))).astype(BF16)


def unpack(coded):
    coded = coded.astype(F32)
    size = lax.rsqrt(lax.rsqrt(jnp.maximum(jnp.abs(coded), FLOOR))) * (1.0 / CODE)
    return jnp.where(coded < 0.0, -size, size)


def pack_square(value):
    return (value * jnp.abs(value)).astype(BF16)


def unpack_square(coded):
    coded = coded.astype(F32)
    return coded * lax.rsqrt(jnp.maximum(jnp.abs(coded), FLOOR))


def step_kernel(
    acts_hbm, enc_hbm, enc_bias, dec_hbm, dec_bias,
    g_out, p_out, d_out, low_sum, plow_sum,
    acts, enc, dec, dec_t, gath, codes, low, plow,
    sums1, sums2, active,
    full3, send3, crecv, xsend, xrecv, zsend3, zrecv3, zb_send, zb_recv, xb_send, xb_recv, keep3, keep_rest, norm_row, norm_wide, factor, code_sum, spread, products,
    ssem, rsem, lsem, osem,
):
    a = lax.axis_index("layer")
    b = lax.axis_index("latent")
    zl, y = a // 4, a % 4
    x, zh, c = b // 4, (b // 2) % 2, b % 2

    def ydev(d):
        return (zl * 4 + (y + d) % 4, b)

    zldev = ((1 - zl) * 4 + y, b)

    def xdev(d):
        return (a, ((x + d) % 4) * 4 + zh * 2 + c)

    zhdev = (a, x * 4 + (1 - zh) * 2 + c)
    cdev = (a, x * 4 + zh * 2 + 1 - c)

    barrier = pltpu.get_barrier_semaphore()
    peers = [zldev, zhdev, cdev] + [ydev(d) for d in (1, 2, 3)] + [xdev(d) for d in (1, 2, 3)]
    for peer in peers:
        pl.semaphore_signal(barrier, inc=1, device_id=peer, device_id_type=MESH)
    load_acts = pltpu.make_async_copy(acts_hbm, acts, lsem.at[2])
    load_enc = pltpu.make_async_copy(enc_hbm, enc, lsem.at[0])
    load_dec = pltpu.make_async_copy(dec_hbm, dec, lsem.at[1])
    load_acts.start()
    load_enc.start()
    load_dec.start()
    load_acts.wait()
    pl.semaphore_wait(barrier, len(peers))

    def push(sem, k, src, dst, device):
        pltpu.make_async_remote_copy(
            src_ref=src, dst_ref=dst, send_sem=ssem.at[sem, k], recv_sem=rsem.at[sem, k],
            device_id=device, device_id_type=MESH,
        ).start()

    def arrived(sem, k, ref):
        pltpu.make_async_copy(ref, ref, rsem.at[sem, k]).wait()

    def gone(sem, k, ref):
        pltpu.make_async_copy(ref, ref, ssem.at[sem, k]).wait()

    left, right = pl.ds(0, HALF), pl.ds(HALF, HALF)
    lower, upper = pl.ds(0, PART), pl.ds(PART, PART)
    mine = pl.ds(aligned(zh * PART, PART), PART)
    theirs = pl.ds(aligned((1 - zh) * PART, PART), PART)

    def sum_send(sem, k, bufs, part):
        send, ya, zb = bufs["send"], bufs["ya"], bufs["zb"]
        if part == 0:
            for d in FAR_FIRST:
                push(sem, k, send.at[k, (y + d) % 4, :, :, left], ya.at[k, d - 1], ydev(d))
        else:
            push(sem + 1, k, send.at[k, :, 1 - zl, :, right], zb.at[k], zldev)

    def sum_mid(sem, k, bufs, narrow, wide):
        full, ya, zb, za_send, za, mid, mid_f32, yb, keep = (
            bufs[n] for n in ("full", "ya", "zb", "za_send", "za", "mid", "mid_f32", "yb", "keep")
        )
        arrived(sem + 1, k, zb.at[k])
        value = full[k % 2, :, zl, :, right] + wide(zb[k])
        mid_f32[k % 2] = value
        mid[k] = narrow(value)
        for d in FAR_FIRST:
            push(sem + 3, k, mid.at[k, (y + d) % 4], yb.at[k, d - 1], ydev(d))
        arrived(sem, k, ya.at[k])

        def total(half):
            value = full[k % 2, y, half, :, left]
            for d in range(3):
                value = value + wide(ya[k, d, half])
            return value

        za_send[k] = narrow(total(1 - zl))
        push(sem + 2, k, za_send.at[k], za.at[k], zldev)
        keep[k % 2] = total(zl)

    def sum_end(sem, k, bufs, wide):
        za, mid_f32, yb, keep = (bufs[n] for n in ("za", "mid_f32", "yb", "keep"))
        arrived(sem + 3, k, yb.at[k])
        second = mid_f32[k % 2, y]
        for d in range(3):
            second = second + wide(yb[k, d])
        arrived(sem + 2, k, za.at[k])
        return keep[k % 2] + wide(za[k]), second

    def spread_send(sem, k, buf):
        own, first = buf.at[k, y, zl], buf.at[k, y, zl, :, left]
        push(sem, k, first, first, zldev)
        for d in FAR_FIRST:
            push(sem + 2, k, own, own, ydev(d))

    def spread_mid(sem, k, buf):
        first = buf.at[k, y, 1 - zl, :, left]
        arrived(sem, k, first)
        for d in FAR_FIRST:
            push(sem + 1, k, first, first, ydev(d))
        arrived(sem + 2, k, buf.at[k, pl.ds(0, 3), 0])
        column = buf.at[k, :, zl, :, right]
        push(sem + 3, k, column, column, zldev)

    def spread_end(sem, k, buf):
        arrived(sem + 1, k, buf.at[k, pl.ds(0, 3), 0, :, left])
        arrived(sem + 3, k, buf.at[k, :, 0, :, right])

    def m0(pair):
        k = 2 * pair
        gath[k + zh, c, x] = acts[pl.ds(aligned(k * 8, 16), 16), :]
        ref = gath.at[k + zh, c, x]
        push(0, k, ref, ref, zhdev)
        for d in FAR_FIRST:
            push(1, k, ref, ref, xdev(d))

    def m1(pair):
        k = 2 * pair
        ref = gath.at[k + 1 - zh, c, x]
        arrived(0, k, ref)
        for d in FAR_FIRST:
            push(1, k, ref, ref, xdev(d))

    def m2(pair):
        k = 2 * pair
        arrived(1, k, gath.at[pl.ds(k, 2), 0, pl.ds(0, 3)])
        ref = gath.at[pl.ds(k, 2), c]
        push(2, k, ref, ref, cdev)

    def wait_pair(k):
        arrived(2, k, gath.at[pl.ds(k, 2), 1 - c])

    def m3(k):
        pl.when(k % 2 == 0)(functools.partial(wait_pair, k))
        pltpu.make_async_copy(gath.at[k], g_out.at[k], osem.at[0]).start()

        for part, cols in enumerate((left, right)):
            rows = gath[k].reshape(ROWS, WIDTH)
            value = jnp.dot(rows, enc[:, cols], preferred_element_type=F32).reshape(4, 2, 16, HALF)
            sums1["full"][k % 2, :, :, :, cols] = value
            sums1["send"][k, :, :, :, cols] = pack(value)
            sum_send(3, k, sums1, part)

    def m4(k):
        sum_mid(3, k, sums1, pack, unpack)

    def m5(k):
        for value, cols in zip(sum_end(3, k, sums1, unpack), (left, right)):
            value = jnp.maximum(value + enc_bias[:, cols], 0.0)
            active[k, :, cols] = value
            codes[k, y, zl, :, cols] = (value * value).astype(BF16)
        spread_send(7, k, codes)

    def m6(k):
        spread_mid(7, k, codes)

    def add_rows(total, k, rows):
        part = jnp.sum(rows.astype(F32).reshape(ROWS // 8, 8, rows.shape[1]), axis=0)
        total[...] = jnp.where(k == 0, part, total[...] + part)

    def m7(k):
        spread_end(7, k, codes)

        def tile(n, _):
            cols = pl.ds(aligned(n * TILE, TILE), TILE)
            rows = codes[k].reshape(ROWS, LATS)
            value = jnp.dot(rows, dec[:, cols], preferred_element_type=F32).reshape(2, 4, 16, TILE)
            full3[k % 2, :, :, :, cols] = value
            send3[k, :, :, :, cols] = value.astype(BF16)
            return 0

        lax.fori_loop(0, WIDTH // TILE, tile, 0)
        push(11, k, send3.at[k, 1 - c], crecv.at[k], cdev)
        add_rows(code_sum, k, codes[k].reshape(ROWS, LATS))

        @pl.when(k == CHUNKS - 1)
        def _():
            total = jnp.sum(code_sum[...], axis=0, keepdims=True) * (PENALTY * SCALE)
            factor[...] = jnp.broadcast_to(total, (128, LATS)).T / norm_wide[...]

    def pair_sum(k, block, cols):
        return full3[k % 2, c, block, :, cols] + crecv[k, block, :, cols].astype(F32)

    def first_of(half):
        return pl.ds(aligned(half * PART, PART), FIRST)

    def rest_of(half):
        return pl.ds(aligned(half * PART + FIRST, REST), REST)

    def m8(k):
        arrived(11, k, crecv.at[k])
        for d in FAR_FIRST:
            to = (x + d) % 4
            for half in range(2):
                xsend[k, d - 1, :, pl.ds(half * FIRST, FIRST)] = pair_sum(k, to, first_of(half)).astype(BF16)
            push(12, k, xsend.at[k, d - 1], xrecv.at[k, d - 1], xdev(d))
        for block in range(4):
            zb_send[k, block] = pair_sum(k, block, rest_of(1 - zh)).astype(BF16)
        push(25, k, zb_send.at[k], zb_recv.at[k], zhdev)

    def m9(k):
        arrived(25, k, zb_recv.at[k])
        for d in FAR_FIRST:
            to = (x + d) % 4
            value = pair_sum(k, to, rest_of(zh)) + zb_recv[k, to].astype(F32)
            xb_send[k, d - 1] = value.astype(BF16)
            push(26, k, xb_send.at[k, d - 1], xb_recv.at[k, d - 1], xdev(d))
        keep_rest[k % 2] = pair_sum(k, x, rest_of(zh)) + zb_recv[k, x].astype(F32)
        arrived(12, k, xrecv.at[k])

        def total(half):
            value = pair_sum(k, x, first_of(half))
            for d in range(3):
                value = value + xrecv[k, d, :, pl.ds(aligned(half * FIRST, FIRST), FIRST)].astype(F32)
            return value

        zsend3[k] = total(1 - zh).astype(BF16)
        push(13, k, zsend3.at[k], zrecv3.at[k], zhdev)
        keep3[k % 2] = total(zh)

    def m10(k):
        arrived(26, k, xb_recv.at[k])
        rest = keep_rest[k % 2]
        for d in range(3):
            rest = rest + xb_recv[k, d].astype(F32)
        arrived(13, k, zrecv3.at[k])
        first = keep3[k % 2] + zrecv3[k].astype(F32)
        for recon, cols in ((first, first_of(zh)), (rest, rest_of(zh))):
            flat = gath[k, c, x, :, cols].astype(F32)
            low[k, c, x, :, cols] = ((recon + dec_bias[:, cols] - flat) * SCALE).astype(BF16)
        ref = low.at[k, c, x, :, mine]
        push(14, k, ref, ref, zhdev)
        for d in FAR_FIRST:
            push(15, k, ref, ref, xdev(d))

    def m11(k):
        ref = low.at[k, c, x, :, theirs]
        arrived(14, k, ref)
        for d in FAR_FIRST:
            push(15, k, ref, ref, xdev(d))

    def m12(k):
        arrived(15, k, low.at[k, 0, pl.ds(0, 3)])
        ref = low.at[k, c]
        push(16, k, ref, ref, cdev)

    def m13(k):
        arrived(16, k, low.at[k, 1 - c])

        for part, cols in enumerate((left, right)):
            rows = low[k].reshape(ROWS, WIDTH)
            value = jnp.dot(rows, dec_t[:, cols], preferred_element_type=F32)
            value = (value + (PENALTY * SCALE) * norm_row[0:1, cols]).reshape(4, 2, 16, HALF)
            sums2["full"][k % 2, :, :, :, cols] = value
            sums2["send"][k, :, :, :, cols] = pack_square(value)
            sum_send(17, k, sums2, part)
        add_rows(low_sum, k, low[k].reshape(ROWS, WIDTH))

    def m14(k):
        sum_mid(17, k, sums2, pack_square, unpack_square)

    def m15(k):
        for value, cols in zip(sum_end(17, k, sums2, unpack_square), (left, right)):
            plow[k, y, zl, :, cols] = (value * (2.0 * active[k, :, cols])).astype(BF16)
        spread_send(21, k, plow)

    def m16(k):
        spread_mid(21, k, plow)

    def m17(k):
        spread_end(21, k, plow)
        pltpu.make_async_copy(plow.at[k], p_out.at[k], osem.at[1]).start()
        add_rows(plow_sum, k, plow[k].reshape(ROWS, LATS))

    def prepare(n):
        rows = pl.ds(aligned(n * 128, 128), 128)
        block = dec[rows, :]
        value = block.astype(F32)
        norm = jnp.sqrt(jnp.sum(value * value, axis=1, keepdims=True) + EPS)
        wide = jnp.broadcast_to(norm, (128, 128))
        norm_wide[rows, :] = wide
        norm_row[:, rows] = wide.T[0:8, :]
        dec_t[:, rows] = block.T

    lines = LATS * (WIDTH // 128) // 4

    def product_out(n):
        part = pl.ds(aligned(n * lines, lines), lines)
        return part, pltpu.make_async_copy(products.at[part], d_out.at[part], osem.at[2])

    def decoder_product(n):
        rows = pl.ds(aligned(n * (LATS // 4), LATS // 4), LATS // 4)
        left_side = codes[:, :, :, :, rows].reshape(TOKENS, LATS // 4)
        for half in range(2):
            right_side = low[:, :, :, :, pl.ds(half * PART, PART)].reshape(TOKENS, PART)
            value = rows_dot(left_side, right_side)
            for j in range(PART // 128):
                at = half * (PART // 128) + j
                part = value[:, j * 128 : (j + 1) * 128]
                part = part + factor[rows, :] * dec[rows, pl.ds(at * 128, 128)].astype(F32)
                spread[pl.ds(at, LATS // 4, stride=WIDTH // 128), :] = part
        part, out = product_out(n)
        products[part, :] = spread[...].astype(BF16)
        out.start()

    stages = [m0, m1, m2, m3, m4, m5, m6, m7, m8, m9, m10, m11, m12, m13, m14, m15, m16, m17]

    def iteration(t, _):
        for m in ORDER:
            k = t - LAGS[m]
            if m == 3:
                pl.when(k == 0)(load_enc.wait)
            ready = jnp.logical_and(k >= 0, k < CHUNKS)
            if m < 3:
                ready = jnp.logical_and(ready, k % 2 == 0)
            pl.when(ready)(functools.partial(stages[m], k // 2 if m < 3 else k))
        @pl.when(jnp.logical_and(t >= FULL, t < FULL + 4))
        def _():
            decoder_product(t - FULL)

        pl.when(t == 0)(load_dec.wait)

        @pl.when(t < 4)
        def _():
            prepare(2 * t)
            prepare(2 * t + 1)

        return 0

    lax.fori_loop(0, CHUNKS + LAGS[-1], iteration, 0)

    def drain(k, _):
        @pl.when(k % 2 == 0)
        def _():
            gone(0, k, gath.at[k, 0, 0])
            gone(1, k, gath.at[pl.ds(k, 2), 0, pl.ds(0, 3)])
            gone(2, k, gath.at[pl.ds(k, 2), 0])

        for sem, bufs in ((3, sums1), (17, sums2)):
            gone(sem, k, bufs["ya"].at[k])
            gone(sem + 1, k, bufs["zb"].at[k])
            gone(sem + 2, k, bufs["za"].at[k])
            gone(sem + 3, k, bufs["yb"].at[k])
        for sem, buf in ((7, codes), (21, plow)):
            gone(sem, k, buf.at[k, 0, 0, :, left])
            gone(sem + 1, k, buf.at[k, pl.ds(0, 3), 0, :, left])
            gone(sem + 2, k, buf.at[k, pl.ds(0, 3), 0])
            gone(sem + 3, k, buf.at[k, :, 0, :, left])
        gone(11, k, crecv.at[k])
        gone(12, k, xsend.at[k])
        gone(13, k, zsend3.at[k])
        gone(14, k, low.at[k, 0, 0, :, lower])
        gone(25, k, zb_send.at[k])
        gone(26, k, xb_send.at[k])
        gone(15, k, low.at[k, 0, pl.ds(0, 3)])
        gone(16, k, low.at[k, 0])
        return 0

    lax.fori_loop(0, CHUNKS, drain, 0)
    pltpu.make_async_copy(gath, g_out, osem.at[0]).wait()
    pltpu.make_async_copy(plow, p_out, osem.at[1]).wait()
    pltpu.make_async_copy(products, d_out, osem.at[2]).wait()


def layer_sum():
    V = pltpu.VMEM
    return {
        "full": V((2, 4, 2, 16, LATS), F32),
        "send": V((CHUNKS, 4, 2, 16, LATS), BF16),
        "ya": V((CHUNKS, 3, 2, 16, HALF), BF16),
        "zb": V((CHUNKS, 4, 16, HALF), BF16),
        "za_send": V((CHUNKS, 16, HALF), BF16),
        "za": V((CHUNKS, 16, HALF), BF16),
        "mid": V((CHUNKS, 4, 16, HALF), BF16),
        "mid_f32": V((2, 4, 16, HALF), F32),
        "yb": V((CHUNKS, 3, 16, HALF), BF16),
        "keep": V((2, 16, HALF), F32),
    }


def exchange(acts, enc, enc_bias, dec, dec_bias):
    any_spec = pl.BlockSpec(memory_space=pl.ANY)
    vmem = pl.BlockSpec(memory_space=pltpu.VMEM)
    V = pltpu.VMEM
    by_latent = (CHUNKS, 2, 4, 16, WIDTH)
    by_layer = (CHUNKS, 4, 2, 16, LATS)
    return pl.pallas_call(
        step_kernel,
        out_shape=[
            jax.ShapeDtypeStruct(by_latent, BF16),
            jax.ShapeDtypeStruct(by_layer, BF16),
            jax.ShapeDtypeStruct((LATS * (WIDTH // 128), 128), BF16),
            jax.ShapeDtypeStruct((8, WIDTH), F32),
            jax.ShapeDtypeStruct((8, LATS), F32),
        ],
        in_specs=[any_spec, any_spec, vmem, any_spec, vmem],
        out_specs=[any_spec, any_spec, any_spec, vmem, vmem],
        scratch_shapes=[
            V((TOKENS // 16, WIDTH), BF16),
            V((WIDTH, LATS), BF16), V((LATS, WIDTH), BF16), V((WIDTH, LATS), BF16),
            V(by_latent, BF16), V(by_layer, BF16), V(by_latent, BF16), V(by_layer, BF16),
            layer_sum(), layer_sum(), V((CHUNKS, 16, LATS), F32),
            V((2, 2, 4, 16, WIDTH), F32), V(by_latent, BF16), V((CHUNKS, 4, 16, WIDTH), BF16),
            V((CHUNKS, 3, 16, 2 * FIRST), BF16), V((CHUNKS, 3, 16, 2 * FIRST), BF16),
            V((CHUNKS, 16, FIRST), BF16), V((CHUNKS, 16, FIRST), BF16),
            V((CHUNKS, 4, 16, REST), BF16), V((CHUNKS, 4, 16, REST), BF16),
            V((CHUNKS, 3, 16, REST), BF16), V((CHUNKS, 3, 16, REST), BF16),
            V((2, 16, FIRST), F32), V((2, 16, REST), F32),
            V((8, LATS), F32), V((LATS, 128), F32), V((LATS, 128), F32), V((8, LATS), F32),
            V((LATS * (WIDTH // 128) // 4, 128), F32), V((LATS * (WIDTH // 128), 128), BF16),
            pltpu.SemaphoreType.DMA((SEMS, CHUNKS)),
            pltpu.SemaphoreType.DMA((SEMS, CHUNKS)),
            pltpu.SemaphoreType.DMA((3,)),
            pltpu.SemaphoreType.DMA((3,)),
        ],
        compiler_params=pltpu.CompilerParams(
            collective_id=0, has_side_effects=True, vmem_limit_bytes=60 << 20
        ),
        name="exchange",
    )(acts, enc, enc_bias, dec, dec_bias)


def rows_dot(left, right):
    return lax.dot_general(left, right, (((0,), (0,)), ((), ())), preferred_element_type=F32)


TILES = 4


def finish_kernel(
    g_hbm, p_hbm, d_hbm, low_sum, plow_sum,
    enc_out, enc_bias_out, dec_out, dec_bias_out,
    g, p, d, enc_stage, dec_stage, lsem, gsem, dsem, esem, wsem,
):
    wide, tall = WIDTH // TILES, LATS * (WIDTH // 128) // TILES
    load_p = pltpu.make_async_copy(p_hbm, p, lsem.at[0])
    load_g, load_d = [], []
    for i in range(TILES):
        cols, rows = pl.ds(i * wide, wide), pl.ds(i * tall, tall)
        load_g.append(pltpu.make_async_copy(g_hbm.at[:, cols], g.at[:, cols], gsem.at[i]))
        load_d.append(pltpu.make_async_copy(d_hbm.at[rows], d.at[rows], dsem.at[i]))
    load_d[0].start()
    load_p.start()
    load_g[0].start()
    enc_bias_out[...] = jnp.sum(plow_sum[...], axis=0, keepdims=True)
    dec_bias_out[...] = jnp.sum(low_sum[...], axis=0, keepdims=True)
    writes = []

    def write(src, dst, sem):
        writes.append(pltpu.make_async_copy(src, dst, sem))
        writes[-1].start()

    for i in range(TILES):
        load_d[i].wait()
        if i + 1 < TILES:
            load_d[i + 1].start()
            load_g[i + 1].start()
        rows = pl.ds(i * tall, tall)
        dec_stage[i] = d[rows, :].astype(F32)
        write(dec_stage.at[i], dec_out.at[rows], wsem.at[i])
        if i == 0:
            load_p.wait()
        load_g[i].wait()
        rows = pl.ds(i * wide, wide)
        enc_stage[i] = rows_dot(g[:, rows], p[...])
        write(enc_stage.at[i], enc_out.at[rows], esem.at[i])
    for copy in writes:
        copy.wait()


def finish(g, p, d, low_sum, plow_sum):
    any_spec = pl.BlockSpec(memory_space=pl.ANY)
    vmem = pl.BlockSpec(memory_space=pltpu.VMEM)
    V = pltpu.VMEM
    lines = LATS * (WIDTH // 128)
    return pl.pallas_call(
        finish_kernel,
        out_shape=[
            jax.ShapeDtypeStruct((WIDTH, LATS), F32),
            jax.ShapeDtypeStruct((1, LATS), F32),
            jax.ShapeDtypeStruct((lines, 128), F32),
            jax.ShapeDtypeStruct((1, WIDTH), F32),
        ],
        in_specs=[any_spec] * 3 + [vmem] * 2,
        out_specs=[any_spec, vmem, any_spec, vmem],
        scratch_shapes=[
            V((TOKENS, WIDTH), BF16), V((TOKENS, LATS), BF16), V((lines, 128), BF16),
            V((TILES, WIDTH // TILES, LATS), F32), V((TILES, lines // TILES, 128), F32),
            pltpu.SemaphoreType.DMA((1,)),
            pltpu.SemaphoreType.DMA((TILES,)),
            pltpu.SemaphoreType.DMA((TILES,)),
            pltpu.SemaphoreType.DMA((TILES,)),
            pltpu.SemaphoreType.DMA((TILES,)),
        ],
        compiler_params=pltpu.CompilerParams(vmem_limit_bytes=56 << 20),
        name="finish",
    )(g, p, d, low_sum, plow_sum)


def on_device(acts, enc_weight, enc_bias, dec_weight, dec_bias):
    dec = dec_weight.reshape(LATS, WIDTH)
    g, p, d, low_sum, plow_sum = exchange(
        acts.reshape(TOKENS // 16, WIDTH), enc_weight.reshape(WIDTH, LATS), enc_bias.reshape(1, LATS), dec, dec_bias
    )
    g, p = g.reshape(TOKENS, WIDTH), p.reshape(TOKENS, LATS)
    enc_grad, enc_bias_grad, dec_grad, dec_bias_grad = finish(g, p, d, low_sum, plow_sum)
    return (
        enc_grad.reshape(1, WIDTH, LATS),
        enc_bias_grad.reshape(LATS),
        dec_grad.reshape(LATS, 1, WIDTH),
        dec_bias_grad,
    )


def solution(mesh):
    return jax.shard_map(
        on_device,
        mesh=mesh,
        in_specs=(
            P("latent", "layer", None),
            P("layer", None, "latent"),
            P("latent"),
            P("latent", "layer", None),
            P("layer", None),
        ),
        out_specs=(
            P("layer", None, "latent"),
            P("latent"),
            P("latent", "layer", None),
            P("layer", None),
        ),
        check_vma=False,
    )
```
